32 devices in a mesh: dom: 8 (over z, y), cls: 4 (over x, core).
Axes of the slice: x: 2, y: 2, z: 4, core: 2. Of those that a mesh axis runs over, the one named last changes fastest.
Arguments:
- images: bfloat16 [1024, 2048], P('dom'), may hold values from -70 to 70
- refs: bfloat16 [100, 12, 2048], P('cls'), may hold values from -0.41992188 to 0.41992188
- ctf: float32 [16, 1024], replicated, may hold values from 0.2 to 1
- inv_noise: float32 [16, 1024], replicated, may hold values from 0.3 to 3
- log_prior: float32 [100], P('cls'), may hold values from -4 to 4
- shifts: int32 [9, 2], replicated, may hold values from -4 to 4
- rot_prior: int32 [1024], P('dom'), may hold values from 0 to 11
- groups: int32 [1024], P('dom'), may hold values from 0 to 15
Outputs:
- new_refs: float32 [100, 24576], P('cls', 'dom')
- loglik: float32 [1024], P('dom')
- class_frac: float32 [100], P('cls')
The draws below stay inside these ranges and needn't reach their ends.
All inputs are finite; a program needn't handle non-finite values.
Results may differ from the reference program's by a relative error of at most 0.005.
Values sent between devices are 32-bit elements; how exact they have to be, the bound alone decides.
No kernel may reach another device: no remote copies, remote signals or barrier semaphores. Data moves between devices by JAX's collectives and lax.ppermute only.
A program may use at most 128 MiB of HBM per device.

```python
import math
import jax
import jax.numpy as jnp
from jax import lax

FPIX = 1024
K = 100
R = 12
S = 9
G = 16
NIMG = 1024


def draw_images(key, part):
    key = jax.random.fold_in(key, 11)
    first = jax.random.fold_in(key, 0)
    values = jnp.clip(jax.random.normal(first, (NIMG, 2 * FPIX), jnp.float32), -6.0, 6.0)
    return values.astype(jnp.bfloat16)


def set_ends(array, rng, smallest, largest):
    shape = array.shape
    spot = [jax.random.randint(jax.random.fold_in(rng, axis), (), 0, shape[axis]) for axis in range(len(shape))]
    array = array.at[tuple(spot)].set(smallest)
    longest = shape.index(max(shape))
    spot[longest] = (spot[longest] + 1) % shape[longest]
    return array.at[tuple(spot)].set(largest)


def block_levels(own_key, shape, pieces, smallest, top_value):
    gain = 1.0
    for position, parts in pieces:
        steps = jax.random.uniform(jax.random.fold_in(jax.random.fold_in(own_key, 6), position), (parts,), jnp.float32, smallest / len(pieces), top_value / len(pieces))
        gain = gain * jnp.repeat(jnp.exp(steps), shape[position] // parts).reshape((-1,) + (1,) * (len(shape) - 1 - position))
    return gain


def gaussian(own_key, extent, deviation, reach, cuts=(), kind=jnp.bfloat16):
    array = jax.random.normal(own_key, extent, jnp.float32) * deviation
    if len(cuts) > 0:
        array = block_levels(own_key, extent, cuts, -0.22, 0.18) * array
    return jnp.clip(array, min=-reach, max=reach).astype(kind)


def setup_inputs(seed: int = 0) -> dict:
    arg_keys = jax.random.split(jax.random.key(seed), 9)
    return {
        "images": draw_images(jax.random.fold_in(arg_keys[8], 71), 0),
        "refs": gaussian(arg_keys[1], (K, R, 2 * FPIX), 0.07, 0.41992188, ((0, 4),)),
        "ctf": jnp.clip(jax.random.uniform(arg_keys[2], (G, FPIX), jnp.float32, 0.2, 1.0), 0.2, 1.0),
        "inv_noise": jnp.clip(jnp.exp(jax.random.uniform(arg_keys[3], (G, FPIX), jnp.float32, math.log(0.3), math.log(3.0))), 0.3, 3.0),
        "log_prior": gaussian(arg_keys[4], (K,), 1.0, 4.0, ((0, 4),), jnp.float32),
        "shifts": set_ends(jax.random.randint(arg_keys[5], (S, 2), -4, 5), jax.random.fold_in(arg_keys[5], 1), -4, 4).astype(jnp.int32),
        "rot_prior": set_ends(jax.random.randint(arg_keys[6], (NIMG,), 0, R), jax.random.fold_in(arg_keys[6], 1), 0, R - 1).astype(jnp.int32),
        "groups": set_ends(jax.random.randint(arg_keys[7], (NIMG,), 0, G), jax.random.fold_in(arg_keys[7], 1), 0, G - 1).astype(jnp.int32),
    }


HI = lax.Precision.HIGHEST

def phase_tables(shifts, fpix):
    side = int(math.isqrt(fpix))
    pos = jnp.arange(fpix, dtype=jnp.int32)
    freq_x = (pos % side).astype(jnp.float32)
    freq_y = (pos // side - side // 2).astype(jnp.float32)
    shift_f = shifts.astype(jnp.float32)
    angle = 2.0 * math.pi * (shift_f[:, 0:1] * freq_x[None] + shift_f[:, 1:2] * freq_y[None]) / 256.0
    return (jnp.cos(angle), jnp.sin(angle))

def weighted_copies(images, groups, cw, cosine, sine):
    fpix = cw.shape[1]
    onehot = (groups[:, None] == jnp.arange(cw.shape[0], dtype=jnp.int32)[None]).astype(jnp.float32)
    cw_img = jnp.dot(onehot, cw, precision=HI)
    real_part = images[:, :fpix].astype(jnp.float32)
    imag_part = images[:, fpix:].astype(jnp.float32)
    sr = real_part[:, None] * cosine[None] + imag_part[:, None] * sine[None]
    si = imag_part[:, None] * cosine[None] - real_part[:, None] * sine[None]
    copies = jnp.concatenate([sr * cw_img[:, None], si * cw_img[:, None]], axis=-1)
    return (copies.astype(jnp.bfloat16), onehot)

def ref_norms(refs, c2w):
    fpix = c2w.shape[1]
    flat = refs.astype(jnp.float32).reshape(-1, 2 * fpix)
    power = flat[:, :fpix] ** 2 + flat[:, fpix:] ** 2
    return jnp.dot(c2w, power.T, precision=HI)

def log_weights(cross, norm_img, log_prior, rot_prior, rots):
    ridx = jnp.arange(rots, dtype=jnp.int32)
    gap = jnp.abs(ridx[None] - rot_prior[:, None])
    gap = jnp.minimum(gap, rots - gap).astype(jnp.float32)
    penalty = 0.15 * gap * gap
    return cross - 0.5 * norm_img[:, None] + log_prior[None, None, :, None] - penalty[:, None, None, :]

def reference(images, refs, ctf, inv_noise, log_prior, shifts, rot_prior, groups):
    nimg = images.shape[0]
    classes, rots, two_f = refs.shape
    fpix = two_f // 2
    ngroup = ctf.shape[0]
    nshift = shifts.shape[0]
    cw = ctf * inv_noise
    c2w = ctf * ctf * inv_noise
    cosine, sine = phase_tables(shifts, fpix)
    norms = ref_norms(refs, c2w)
    flat_refs = refs.reshape(classes * rots, two_f)
    block = min(512, nimg)
    steps_n = nimg // block

    def one_block(carry, idx):
        num, mass = carry
        start = (idx * block).astype(jnp.int32)
        img = lax.dynamic_slice_in_dim(images, start, block, 0)
        grp = lax.dynamic_slice_in_dim(groups, start, block, 0)
        rp = lax.dynamic_slice_in_dim(rot_prior, start, block, 0)
        copies, onehot = weighted_copies(img, grp, cw, cosine, sine)
        rows = copies.reshape(block * nshift, two_f)
        cross = jnp.dot(rows, flat_refs.T, preferred_element_type=jnp.float32).reshape(block, nshift, classes, rots)
        norm_img = jnp.dot(onehot, norms, precision=HI).reshape(block, 1, classes, rots)
        logp = log_weights(cross, norm_img[:, 0], log_prior, rp, rots)
        peak = lax.optimization_barrier(jnp.max(logp, axis=(1, 2, 3)))
        total = lax.optimization_barrier(jnp.sum(jnp.exp(logp - peak[:, None, None, None]), axis=(1, 2, 3)))
        loglik = peak + jnp.log(total)
        post = jnp.exp(logp - loglik[:, None, None, None]).astype(jnp.bfloat16)
        post_f = post.astype(jnp.float32)
        num = num + jnp.einsum('nskr,nsq->kqr', post_f, copies.astype(jnp.float32), precision=HI)
        per_img = lax.optimization_barrier(jnp.sum(post_f, axis=1)).reshape(block, classes * rots)
        mass = mass + jnp.dot(onehot.T, per_img, precision=HI)
        return ((num, mass), loglik)
    init = (jnp.zeros((classes, two_f, rots), jnp.float32), jnp.zeros((ngroup, classes * rots), jnp.float32))
    (num, mass), logliks = lax.scan(one_block, init, jnp.arange(steps_n, dtype=jnp.int32))
    c2w_two = jnp.concatenate([c2w, c2w], axis=1)
    den = jnp.einsum('gkr,gq->kqr', mass.reshape(ngroup, classes, rots), c2w_two, precision=HI)
    new_refs = (num / (den + 1.0)).reshape(classes, two_f * rots)
    class_frac = lax.optimization_barrier(jnp.sum(mass.reshape(ngroup, classes, rots), axis=(0, 2))) / nimg
    return (new_refs, logliks.reshape(nimg), class_frac)
```

```python
import math

import jax
import jax.numpy as jnp
from jax import lax
from jax.experimental import pallas as pl
from jax.experimental.pallas import tpu as pltpu
from jax.sharding import PartitionSpec as P

HI = lax.Precision.HIGHEST
F32 = jnp.float32
BF16 = jnp.bfloat16
VMEM = pl.BlockSpec(memory_space=pltpu.VMEM)
HBM = pl.BlockSpec(memory_space=pltpu.HBM)
PARAMS = pltpu.CompilerParams(vmem_limit_bytes=20 * 1024 * 1024)
LOW = -1e30


def round_up(value, multiple):
    return -(-value // multiple) * multiple


def thirds(value, axis):
    high = value.astype(BF16)
    rest = value - high.astype(F32)
    middle = rest.astype(BF16)
    low = (rest - middle.astype(F32)).astype(BF16)
    return jnp.concatenate([high, middle, low], axis=axis)


def estep_kernel(
    images_hbm, refs_hbm, ctf_hbm, inv_hbm, prior_hbm, shifts_hbm, rot_hbm, groups_hbm,
    weight_ref, copies_ref, stats_ref, onehot_ref, share_ref,
    images_ref, refs_ref, ctf_ref, inv_ref, prior_ref, shifts_ref, rot_ref, groups_ref,
    flat_ref, flat_bf_ref, cw_ref, cos_ref, sin_ref, sems,
):
    count, two_f = images_ref.shape
    fpix = two_f // 2
    rots, classes, _ = refs_ref.shape
    ngroup = ctf_ref.shape[0]
    nshift = shifts_ref.shape[1]
    rpad = flat_ref.shape[0]
    half = classes * rots // 2
    hpad = rpad // 2

    loads = [
        pltpu.make_async_copy(src, dst, sems.at[index])
        for index, (src, dst) in enumerate(
            (
                (shifts_hbm, shifts_ref),
                (groups_hbm, groups_ref),
                (ctf_hbm, ctf_ref),
                (inv_hbm, inv_ref),
                (images_hbm, images_ref),
                (refs_hbm, refs_ref),
                (prior_hbm, prior_ref),
                (rot_hbm, rot_ref),
            )
        )
    ]
    for load in loads:
        load.start()
    side = int(math.isqrt(fpix))
    pos = lax.broadcasted_iota(jnp.int32, (1, fpix), 1).astype(F32)
    line = jnp.floor((pos + 0.5) * (1.0 / side))
    freq_x = pos - side * line
    freq_y = line - side // 2
    loads[0].wait()
    index = lax.broadcasted_iota(jnp.int32, (cos_ref.shape[0], 1), 0)
    shift_x = jnp.zeros(index.shape, F32)
    shift_y = jnp.zeros(index.shape, F32)
    for s in range(nshift):
        shift_x = jnp.where(index == s, shifts_ref[0, s].astype(F32), shift_x)
        shift_y = jnp.where(index == s, shifts_ref[1, s].astype(F32), shift_y)
    angle = 2.0 * math.pi * (shift_x * freq_x + shift_y * freq_y) / 256.0
    cos_ref[...] = jnp.cos(angle)
    sin_ref[...] = jnp.sin(angle)

    for load in loads[1:4]:
        load.wait()
    own = groups_ref[...].reshape(1, count)
    onehot = (own == lax.broadcasted_iota(jnp.int32, (ngroup, count), 0)).astype(F32)
    onehot_ref[...] = onehot
    three = jnp.concatenate([onehot] * 3, axis=0).astype(BF16)
    weight = ctf_ref[...] * inv_ref[...]
    cw_ref[...] = lax.dot_general(
        three, thirds(weight, 0), (((0,), (0,)), ((), ())), preferred_element_type=F32
    )
    loads[4].wait()

    def build(shifts):
        for at in range(0, count, 16):
            for lane in range(0, fpix, 128):
                real = images_ref[at : at + 16, lane : lane + 128].astype(F32)
                imag = images_ref[at : at + 16, fpix + lane : fpix + lane + 128].astype(F32)
                cw = cw_ref[at : at + 16, lane : lane + 128]
                for s in shifts:
                    c = cos_ref[s : s + 1, lane : lane + 128]
                    d = sin_ref[s : s + 1, lane : lane + 128]
                    to = s * count + at
                    copies_ref[to : to + 16, lane : lane + 128] = (
                        (real * c + imag * d) * cw
                    ).astype(BF16)
                    copies_ref[to : to + 16, fpix + lane : fpix + lane + 128] = (
                        (imag * c - real * d) * cw
                    ).astype(BF16)

    for load in loads[5:]:
        load.wait()
    for side in range(2):
        flat_ref[side * hpad + half : (side + 1) * hpad, :] = jnp.zeros((hpad - half, two_f), F32)
        for r in range(rots // 2):
            at = side * hpad + r * classes
            flat_ref[at : at + classes, :] = refs_ref[side * (rots // 2) + r].astype(F32)
    power = flat_ref[:, :fpix] ** 2 + flat_ref[:, fpix:] ** 2
    c2w = ctf_ref[...] * ctf_ref[...] * inv_ref[...]
    high = power.astype(BF16)
    low = (power - high.astype(F32)).astype(BF16)
    c2w = thirds(c2w, 0)
    norms = lax.dot_general(
        high, c2w, (((1,), (1,)), ((), ())), preferred_element_type=F32
    ) + lax.dot_general(low, c2w, (((1,), (1,)), ((), ())), preferred_element_type=F32)
    norms = norms[:, :ngroup] + norms[:, ngroup : 2 * ngroup] + norms[:, 2 * ngroup :]
    norm_img = jnp.dot(thirds(norms, 1), three, preferred_element_type=F32)
    row = lax.broadcasted_iota(jnp.int32, (rpad, 1), 0)
    row = jnp.where(row < hpad, row, row - hpad + half)
    valid = (row < half) | ((row >= half) & (lax.broadcasted_iota(jnp.int32, (rpad, 1), 0) >= hpad))
    valid = valid & (row < 2 * half)
    row = row.astype(F32)
    rot = jnp.floor((row + 0.5) * (1.0 / classes))
    lane = lax.broadcasted_iota(jnp.int32, (rpad, classes), 1).astype(F32)
    own = jnp.where(lane == row - rot * classes, prior_ref[...].reshape(1, classes), 0.0)
    prior = jnp.sum(own, axis=1, keepdims=True)
    gap = jnp.abs(rot - rot_ref[...].reshape(1, count).astype(F32))
    gap = jnp.minimum(gap, rots - gap)
    bias = prior - 0.5 * norm_img - 0.15 * gap * gap
    bias = jnp.where(valid, bias, LOW)

    flat_bf_ref[...] = flat_ref[...].astype(BF16)
    total = nshift * count
    pairs = [list(range(s, min(s + 4, nshift))) for s in range(0, nshift, 4)]
    peak = None
    build(pairs[0])
    for index, shifts in enumerate(pairs):
        if index + 1 < len(pairs):
            build(pairs[index + 1])
        at = shifts[0] * count
        cross = lax.dot_general(
            flat_bf_ref[...], copies_ref[at : at + len(shifts) * count, :], (((1,), (1,)), ((), ())),
            preferred_element_type=F32,
        )
        for sub in range(0, len(shifts) * count, count):
            logp = cross[:, sub : sub + count] + bias
            weight_ref[:, at + sub : at + sub + count] = logp
            top = jnp.max(logp, axis=0, keepdims=True)
            peak = top if peak is None else jnp.maximum(peak, top)
    mass = jnp.zeros((rpad, count), F32)
    for at in range(0, total, count):
        value = jnp.exp(weight_ref[:, at : at + count] - peak)
        weight_ref[:, at : at + count] = value
        mass = mass + value
    stats_ref[0:1, :] = peak
    stats_ref[1:2, :] = jnp.sum(mass, axis=0, keepdims=True)

    width = share_ref.shape[1]
    if width % 128 == 0:
        start = pl.multiple_of(lax.rem(lax.axis_index("dom") * width, fpix), width)
        share_ctf = ctf_ref[:, pl.ds(start, width)]
        share_ref[...] = share_ctf * share_ctf * inv_ref[:, pl.ds(start, width)]


def estep(images, refs, ctf, inv_noise, log_prior, shifts, rot_prior, groups, rpad, width):
    count, two_f = images.shape
    ngroup, fpix = ctf.shape
    nshift = shifts.shape[0]
    refs = jnp.swapaxes(refs, 0, 1)
    shifts = shifts.T
    return pl.pallas_call(
        estep_kernel,
        out_shape=(
            jax.ShapeDtypeStruct((rpad, nshift * count), F32),
            jax.ShapeDtypeStruct((nshift * count, two_f), BF16),
            jax.ShapeDtypeStruct((2, count), F32),
            jax.ShapeDtypeStruct((ngroup, count), F32),
            jax.ShapeDtypeStruct((ngroup, width), F32),
        ),
        in_specs=[HBM] * 8,
        out_specs=(VMEM,) * 5,
        scratch_shapes=[
            pltpu.VMEM(images.shape, images.dtype),
            pltpu.VMEM(refs.shape, refs.dtype),
            pltpu.VMEM(ctf.shape, F32),
            pltpu.VMEM(ctf.shape, F32),
            pltpu.VMEM(log_prior.shape, F32),
            pltpu.SMEM(shifts.shape, jnp.int32),
            pltpu.VMEM(rot_prior.shape, jnp.int32),
            pltpu.VMEM(groups.shape, jnp.int32),
            pltpu.VMEM((rpad, two_f), F32),
            pltpu.VMEM((rpad, two_f), BF16),
            pltpu.VMEM((count, fpix), F32),
            pltpu.VMEM((round_up(nshift, 8), fpix), F32),
            pltpu.VMEM((round_up(nshift, 8), fpix), F32),
            pltpu.SemaphoreType.DMA((8,)),
        ],
        compiler_params=PARAMS,
        name="estep",
    )(
        *(
            pltpu.with_memory_space_constraint(value, pltpu.HBM)
            for value in (images, refs, ctf, inv_noise, log_prior, shifts, rot_prior, groups)
        )
    )


def posterior(stats_refs, weight_ref, onehot_ref, post_ref, loglik_ref):
    count = onehot_ref.shape[1]
    parts = len(stats_refs)
    me = lax.axis_index("cls")
    stats = [ref[...] for ref in stats_refs]
    ordered = []
    for place in range(parts):
        value = stats[0]
        for ahead in range(1, parts):
            value = jnp.where(lax.rem(me + ahead, parts) == place, stats[ahead], value)
        ordered.append(value)
    peak = ordered[0][0:1]
    for value in ordered[1:]:
        peak = jnp.maximum(peak, value[0:1])
    total = jnp.zeros_like(peak)
    for value in ordered:
        total = total + value[1:2] * jnp.exp(value[0:1] - peak)
    loglik = peak + jnp.log(total)
    scale = jnp.exp(stats[0][0:1] - loglik)
    loglik_ref[...] = loglik.reshape(count)
    per_img = None
    for at in range(0, weight_ref.shape[1], count):
        post = (weight_ref[:, at : at + count] * scale).astype(BF16)
        post_ref[:, at : at + count] = post
        post = post.astype(F32)
        per_img = post if per_img is None else per_img + post
    three = jnp.concatenate([onehot_ref[...]] * 3, axis=1).astype(BF16)
    hpad = per_img.shape[0] // 2
    return [
        lax.dot_general(
            three, thirds(per_img[at : at + hpad], 1), (((1,), (1,)), ((), ())),
            preferred_element_type=F32,
        )
        for at in (0, hpad)
    ]


def class_sums(post_ref, copies_ref, rows, at, width):
    return jnp.dot(post_ref[rows, :], copies_ref[:, pl.ds(at, width)], preferred_element_type=F32)


LINE = 4
PAIR = 2


def owner_column(place, mine, width):
    me = lax.axis_index("dom")
    z = me // PAIR
    y = me % PAIR
    low = z < 2
    stop = [
        jnp.where(low, 3, 0), jnp.where(low, 2, 1), jnp.where(low, 1 - z, 5 - z), z
    ][place]
    side = y if mine else 1 - y
    return pl.multiple_of((stop * PAIR + side) * width, width)


def put_mass(ref, mass):
    ngroup, hpad = mass.shape
    at = ref.shape[0] - ngroup
    ref[at:, 0:hpad] = mass
    ref[at:, hpad:] = jnp.zeros((ngroup, ref.shape[1] - hpad), F32)


def first_kernel(nstat, *refs):
    stats_refs = refs[:nstat]
    weight_ref, copies_ref, onehot_ref, post_ref, send_ref, mass_ref, loglik_ref = refs[nstat:]
    hpad = post_ref.shape[0] // 2
    ngroup = onehot_ref.shape[0]
    width = send_ref.shape[1]
    send = send_ref.shape[0] - ngroup
    mass = posterior(stats_refs, weight_ref, onehot_ref, post_ref, loglik_ref)
    sums = class_sums(post_ref, copies_ref, pl.ds(0, hpad), owner_column(0, False, width), width)
    send_ref[0:send, :] = sums[0:send]
    put_mass(send_ref, mass[0])
    put_mass(mass_ref, mass[1])


def second_kernel(post_ref, copies_ref, mass_ref, send_ref):
    hpad = post_ref.shape[0] // 2
    width = send_ref.shape[1]
    send = send_ref.shape[0] - mass_ref.shape[0]
    sums = class_sums(post_ref, copies_ref, pl.ds(hpad, hpad), owner_column(0, False, width), width)
    send_ref[0:send, :] = sums[0:send]
    send_ref[send:, :] = mass_ref[...]


def rest_kernel(post_ref, copies_ref, send_a_ref, mass_ref, *out_refs):
    hpad = post_ref.shape[0] // 2
    width = mass_ref.shape[1]
    chains = (out_refs[:7], out_refs[7:])
    send = chains[0][1].shape[0]
    for place in (1, 0, 2, 3):
        for mine in (False, True):
            if place == 0 and not mine:
                continue
            at = owner_column(place, mine, width)

            @pl.when(at >= 0)
            def _(at=at, place=place, mine=mine):
                sums = class_sums(post_ref, copies_ref, pl.ds(0, 2 * hpad), at, width)
                for index, refs in enumerate(chains):
                    ref = refs[0] if place == 0 else refs[2 * place - 1 + int(mine)]
                    ref[0:send, :] = sums[index * hpad : index * hpad + send]

    chains[0][0][send:, :] = send_a_ref[send:, :]
    chains[1][0][send:, :] = mass_ref[...]


def last_kernel(chain, classes, rots, images, *refs):
    (keep_ref, pair_ref, own_ref, line_ref, cross_ref, share_ref), refs = refs[:6], refs[6:]
    before, refs = (refs[:2], refs[2:]) if chain else (None, refs)
    new_ref, frac_ref, ratio_ref = refs
    send, width = keep_ref.shape
    mine = rots // 2
    z = lax.axis_index("dom") // PAIR
    end = (z == 0) | (z == LINE - 1)
    mass = jnp.where(end, line_ref[send:, :], own_ref[send:, :])
    den = lax.dot_general(
        mass, share_ref[...], (((0,), (0,)), ((), ())), precision=HI, preferred_element_type=F32
    )
    num = keep_ref[...] + pair_ref[...] + line_ref[0:send, :]
    num = num + jnp.where(end, 0.0, cross_ref[...])
    ratio_ref[0:send, :] = num / (den[0:send] + 1.0)
    ratio_ref[send:, :] = jnp.zeros((ratio_ref.shape[0] - send, width), F32)

    piece = 32
    per = 128 // piece
    kpad = round_up(classes, 8)
    lane = lax.broadcasted_iota(jnp.int32, (kpad, 128), 1)
    tiles = []
    for chunk in range(0, width, piece):
        base = chunk // 128 * 128
        parts = []
        for r0 in range(0, mine, per):
            acc = jnp.zeros((kpad, 128), F32)
            for u in range(min(per, mine - r0)):
                start = (r0 + u) * classes
                values = ratio_ref[start : start + kpad, base : base + 128]
                turn = (u * piece - (chunk - base)) % 128
                if turn:
                    values = pltpu.roll(values, turn, 1)
                acc = jnp.where((lane >= u * piece) & (lane < (u + 1) * piece), values, acc)
            parts.append(acc)
        tiles.append(jnp.concatenate(parts, axis=1))
    wide = piece * rots
    deep = tiles[0].shape[1]
    src = lax.broadcasted_iota(jnp.int32, (deep, wide), 0)
    dst = lax.broadcasted_iota(jnp.int32, (deep, wide), 1)
    src_r = src // piece
    perm = ((src - src_r * piece) * rots + src_r + chain * mine == dst) & (src_r < mine)
    moved = jnp.dot(
        thirds(jnp.concatenate(tiles, axis=0), 0), perm.astype(BF16), preferred_element_type=F32
    )
    count = len(tiles) * kpad
    moved = moved[0:count] + moved[count : 2 * count] + moved[2 * count :]
    for index in range(len(tiles)):
        columns = slice(index * wide, (index + 1) * wide)
        value = moved[index * kpad : index * kpad + classes, :]
        new_ref[:, columns] = value + before[0][:, columns] if before else value
    mrow = lax.broadcasted_iota(jnp.int32, (width, classes), 0)
    mcol = lax.broadcasted_iota(jnp.int32, (width, classes), 1)
    place = mrow.astype(F32)
    place = place - classes * jnp.floor((place + 0.5) * (1.0 / classes))
    member = ((place == mcol.astype(F32)) & (mrow < mine * classes)).astype(F32)
    share = jnp.dot(
        jnp.sum(mass, axis=0, keepdims=True), member, precision=HI, preferred_element_type=F32
    )
    if before:
        share = share + before[1][...]
        frac_ref[...] = (share / images).reshape(classes)
    else:
        frac_ref[...] = share


def line_path(stats, weight, copies, onehot, share, classes, rots, images):
    half = classes * rots // 2
    send = round_up(half, 8)
    ngroup, width = share.shape
    dom_n = lax.axis_size("dom")
    cls_n = lax.axis_size("cls")
    full = jax.ShapeDtypeStruct((send + ngroup, width), F32)
    body = jax.ShapeDtypeStruct((send, width), F32)
    mass_shape = jax.ShapeDtypeStruct((ngroup, width), F32)

    def first(*refs):
        first_kernel(len(stats), *refs)

    post, send_a, mass_b, loglik = pl.pallas_call(
        first,
        out_shape=(
            jax.ShapeDtypeStruct(weight.shape, BF16),
            full,
            mass_shape,
            jax.ShapeDtypeStruct(onehot.shape[1:], F32),
        ),
        in_specs=[VMEM] * (len(stats) + 3),
        out_specs=(VMEM,) * 4,
        compiler_params=PARAMS,
        name="first_sums",
    )(*stats, weight, copies, onehot)
    send_b = pl.pallas_call(
        second_kernel,
        out_shape=full,
        in_specs=[VMEM] * 3,
        out_specs=VMEM,
        compiler_params=PARAMS,
        name="second_sums",
    )(post, copies, mass_b)
    parts = pl.pallas_call(
        rest_kernel,
        out_shape=((full,) + (body,) * 6) * 2,
        in_specs=[VMEM] * 4,
        out_specs=(VMEM,) * 14,
        compiler_params=PARAMS,
        name="rest_sums",
    )(post, copies, send_a, mass_b)

    def along(pairs):
        return [(a * PAIR + y, b * PAIR + y) for a, b in pairs for y in range(PAIR)]

    across = [(d, d ^ 1) for d in range(dom_n)]
    outer = along([(0, 1), (1, 0), (2, 3), (3, 2)])
    facing = {0: 0, 1: 2, 2: 1, 3: 3}
    middle = [
        (
            (a * PAIR + y) * cls_n + c,
            (b * PAIR + y) * cls_n + (c if a != b else c ^ 1),
        )
        for a, b in facing.items()
        for y in range(PAIR)
        for c in range(cls_n)
    ]
    z = lax.axis_index("dom") // PAIR
    inner = (z != 0) & (z != LINE - 1)

    def swap(value):
        return lax.ppermute(value, "dom", across)

    def reduce_chain(send0, keep0, send1, keep1, send2, keep2, send3, keep3):
        pair0 = swap(send0)
        send1, pair0 = lax.optimization_barrier((send1, pair0))
        pair1 = swap(send1)
        send2, pair1 = lax.optimization_barrier((send2, pair1))
        pair2 = swap(send2)
        send3, pair2 = lax.optimization_barrier((send3, pair2))
        pair = swap(send3)
        sum0 = keep0 + pair0
        sum1 = keep1 + pair1
        sum2 = keep2 + pair2
        both0 = sum0 + lax.ppermute(sum0, "dom", outer)
        got1 = lax.ppermute(sum1, "dom", outer)
        got2 = lax.ppermute(both0, ("dom", "cls"), middle)
        to_ends = jnp.concatenate([sum2, both0[send:]], axis=0) + jnp.where(inner, got2, 0.0)
        line = lax.ppermute(to_ends, "dom", outer)
        cross = lax.ppermute(sum1 + got1, ("dom", "cls"), middle)
        return keep3, pair, to_ends, line, cross

    chain_a = reduce_chain(send_a, *parts[:7])
    chain_b = reduce_chain(send_b, *parts[7:])
    before = ()
    for chain, pieces in enumerate((chain_a, chain_b)):

        def last(*refs, chain=chain):
            last_kernel(chain, classes, rots, images, *refs)

        before = pl.pallas_call(
            last,
            out_shape=(
                jax.ShapeDtypeStruct((classes, width * rots), F32),
                jax.ShapeDtypeStruct((classes,) if chain else (1, classes), F32),
            ),
            in_specs=[VMEM] * (6 + len(before)),
            out_specs=(VMEM, VMEM),
            scratch_shapes=[pltpu.VMEM((send + 16, width), F32)],
            compiler_params=PARAMS,
            name="last_ratio",
        )(*pieces, share, *before)
    return before[0], loglik, before[1]


def plain_path(stats, weight, copies, onehot, ctf, inv_noise, classes, rots, images):
    rpad = weight.shape[0]
    hpad = rpad // 2
    half = classes * rots // 2
    ngroup, fpix = ctf.shape
    two_f = 2 * fpix
    dom_n = lax.axis_size("dom")
    width = two_f // dom_n
    nstat = len(stats)

    def sums(*refs):
        weight_ref, copies_ref, onehot_ref, num_ref, mass_ref, loglik_ref, post_ref = refs[nstat:]
        mass = posterior(refs[:nstat], weight_ref, onehot_ref, post_ref, loglik_ref)
        mass_ref[0] = mass[0]
        mass_ref[1] = mass[1]
        for at in range(0, two_f, 256):
            num_ref[:, at : at + 256] = class_sums(
                post_ref, copies_ref, pl.ds(0, rpad), at, 256
            )

    num, mass, loglik = pl.pallas_call(
        sums,
        out_shape=(
            jax.ShapeDtypeStruct((rpad, two_f), F32),
            jax.ShapeDtypeStruct((2, ngroup, hpad), F32),
            jax.ShapeDtypeStruct(onehot.shape[1:], F32),
        ),
        in_specs=[VMEM] * (len(stats) + 3),
        out_specs=(VMEM,) * 3,
        scratch_shapes=[pltpu.VMEM(weight.shape, BF16)],
        compiler_params=PARAMS,
        name="all_sums",
    )(*stats, weight, copies, onehot)
    mass = jnp.concatenate([mass[0, :, :half], mass[1, :, :half]], axis=1)
    mass = lax.psum(mass, "dom")
    num = jnp.concatenate([num[:half], num[hpad : hpad + half]], axis=0)
    num = lax.psum_scatter(num, "dom", scatter_dimension=1, tiled=True)
    c2w = ctf * ctf * inv_noise
    c2w_two = jnp.concatenate([c2w, c2w], axis=1)
    c2w_part = lax.dynamic_slice_in_dim(c2w_two, lax.axis_index("dom") * width, width, 1)
    den = jnp.einsum("gn,gq->nq", mass, c2w_part, precision=HI)
    ratio = (num / (den + 1.0)).reshape(rots, classes, width)
    new_refs = ratio.transpose(1, 2, 0).reshape(classes, width * rots)
    frac = jnp.sum(mass.reshape(ngroup, rots, classes), axis=(0, 1)) / images
    return new_refs, loglik, frac


def local(images, refs, ctf, inv_noise, log_prior, shifts, rot_prior, groups):
    classes, rots, two_f = refs.shape
    half = classes * rots // 2
    hpad = round_up(half, 16)
    count = images.shape[0]
    ngroup = ctf.shape[0]
    dom_n = lax.axis_size("dom")
    cls_n = lax.axis_size("cls")
    width = two_f // dom_n
    weight, copies, stat, onehot, share = estep(
        images, refs, ctf, inv_noise, log_prior, shifts, rot_prior, groups, 2 * hpad, width
    )
    stats = [stat] + [
        lax.ppermute(stat, "cls", [((c + ahead) % cls_n, c) for c in range(cls_n)])
        for ahead in range(1, cls_n)
    ]
    fits = (
        dom_n == LINE * PAIR
        and cls_n % 2 == 0
        and width % 128 == 0
        and hpad <= width
        and ngroup % 8 == 0
    )
    images_n = count * dom_n
    if fits:
        return line_path(stats, weight, copies, onehot, share, classes, rots, images_n)
    return plain_path(stats, weight, copies, onehot, ctf, inv_noise, classes, rots, images_n)


def solution(mesh):
    return jax.shard_map(
        local,
        mesh=mesh,
        in_specs=(
            P("dom", None),
            P("cls", None, None),
            P(),
            P(),
            P("cls"),
            P(),
            P("dom"),
            P("dom"),
        ),
        out_specs=(P("cls", "dom"), P("dom"), P("cls")),
        check_vma=False,
    )
```

```python
import math

import jax
import jax.numpy as jnp
from jax import lax
from jax.experimental import pallas as pl
from jax.experimental.pallas import tpu as pltpu
from jax.sharding import PartitionSpec as P

HI = lax.Precision.HIGHEST
F32 = jnp.float32
BF16 = jnp.bfloat16
VMEM = pl.BlockSpec(memory_space=pltpu.VMEM)
HBM = pl.BlockSpec(memory_space=pltpu.HBM)
PARAMS = pltpu.CompilerParams(vmem_limit_bytes=20 * 1024 * 1024)
LOW = -1e30


def round_up(value, multiple):
    return -(-value // multiple) * multiple


def thirds(value, axis):
    high = value.astype(BF16)
    rest = value - high.astype(F32)
    middle = rest.astype(BF16)
    low = (rest - middle.astype(F32)).astype(BF16)
    return jnp.concatenate([high, middle, low], axis=axis)


def estep_kernel(
    images_hbm, refs_hbm, ctf_hbm, inv_hbm, prior_hbm, shifts_hbm, rot_hbm, groups_hbm,
    weight_ref, copies_ref, stats_ref, onehot_ref, share_ref,
    images_ref, refs_ref, ctf_ref, inv_ref, prior_ref, shifts_ref, rot_ref, groups_ref,
    flat_ref, flat_bf_ref, cw_ref, cos_ref, sin_ref, sems,
):
    count, two_f = images_ref.shape
    fpix = two_f // 2
    rots, classes, _ = refs_ref.shape
    ngroup = ctf_ref.shape[0]
    nshift = shifts_ref.shape[1]
    rpad = flat_ref.shape[0]
    half = classes * rots // 2
    hpad = rpad // 2

    loads = [
        pltpu.make_async_copy(src, dst, sems.at[index])
        for index, (src, dst) in enumerate(
            (
                (shifts_hbm, shifts_ref),
                (groups_hbm, groups_ref),
                (ctf_hbm, ctf_ref),
                (inv_hbm, inv_ref),
                (images_hbm, images_ref),
                (refs_hbm, refs_ref),
                (prior_hbm, prior_ref),
                (rot_hbm, rot_ref),
            )
        )
    ]
    for load in loads:
        load.start()
    side = int(math.isqrt(fpix))
    pos = lax.broadcasted_iota(jnp.int32, (1, fpix), 1).astype(F32)
    line = jnp.floor((pos + 0.5) * (1.0 / side))
    freq_x = pos - side * line
    freq_y = line - side // 2
    loads[0].wait()
    index = lax.broadcasted_iota(jnp.int32, (cos_ref.shape[0], 1), 0)
    shift_x = jnp.zeros(index.shape, F32)
    shift_y = jnp.zeros(index.shape, F32)
    for s in range(nshift):
        shift_x = jnp.where(index == s, shifts_ref[0, s].astype(F32), shift_x)
        shift_y = jnp.where(index == s, shifts_ref[1, s].astype(F32), shift_y)
    angle = 2.0 * math.pi * (shift_x * freq_x + shift_y * freq_y) / 256.0
    cos_ref[...] = jnp.cos(angle)
    sin_ref[...] = jnp.sin(angle)

    for load in loads[1:4]:
        load.wait()
    own = groups_ref[...].reshape(1, count)
    onehot = (own == lax.broadcasted_iota(jnp.int32, (ngroup, count), 0)).astype(F32)
    onehot_ref[...] = onehot
    three = jnp.concatenate([onehot] * 3, axis=0).astype(BF16)
    weight = ctf_ref[...] * inv_ref[...]
    cw_ref[...] = lax.dot_general(
        three, thirds(weight, 0), (((0,), (0,)), ((), ())), preferred_element_type=F32
    )
    loads[4].wait()

    def build(shifts):
        for at in range(0, count, 16):
            for lane in range(0, fpix, 128):
                real = images_ref[at : at + 16, lane : lane + 128].astype(F32)
                imag = images_ref[at : at + 16, fpix + lane : fpix + lane + 128].astype(F32)
                cw = cw_ref[at : at + 16, lane : lane + 128]
                for s in shifts:
                    c = cos_ref[s : s + 1, lane : lane + 128]
                    d = sin_ref[s : s + 1, lane : lane + 128]
                    to = s * count + at
                    copies_ref[to : to + 16, lane : lane + 128] = (
                        (real * c + imag * d) * cw
                    ).astype(BF16)
                    copies_ref[to : to + 16, fpix + lane : fpix + lane + 128] = (
                        (imag * c - real * d) * cw
                    ).astype(BF16)

    for load in loads[5:]:
        load.wait()
    for side in range(2):
        flat_ref[side * hpad + half : (side + 1) * hpad, :] = jnp.zeros((hpad - half, two_f), F32)
        for r in range(rots // 2):
            at = side * hpad + r * classes
            flat_ref[at : at + classes, :] = refs_ref[side * (rots // 2) + r].astype(F32)
    power = flat_ref[:, :fpix] ** 2 + flat_ref[:, fpix:] ** 2
    c2w = ctf_ref[...] * ctf_ref[...] * inv_ref[...]
    high = power.astype(BF16)
    low = (power - high.astype(F32)).astype(BF16)
    c2w = thirds(c2w, 0)
    norms = lax.dot_general(
        high, c2w, (((1,), (1,)), ((), ())), preferred_element_type=F32
    ) + lax.dot_general(low, c2w, (((1,), (1,)), ((), ())), preferred_element_type=F32)
    norms = norms[:, :ngroup] + norms[:, ngroup : 2 * ngroup] + norms[:, 2 * ngroup :]
    norm_img = jnp.dot(thirds(norms, 1), three, preferred_element_type=F32)
    row = lax.broadcasted_iota(jnp.int32, (rpad, 1), 0)
    row = jnp.where(row < hpad, row, row - hpad + half)
    valid = (row < half) | ((row >= half) & (lax.broadcasted_iota(jnp.int32, (rpad, 1), 0) >= hpad))
    valid = valid & (row < 2 * half)
    row = row.astype(F32)
    rot = jnp.floor((row + 0.5) * (1.0 / classes))
    lane = lax.broadcasted_iota(jnp.int32, (rpad, classes), 1).astype(F32)
    own = jnp.where(lane == row - rot * classes, prior_ref[...].reshape(1, classes), 0.0)
    prior = jnp.sum(own, axis=1, keepdims=True)
    gap = jnp.abs(rot - rot_ref[...].reshape(1, count).astype(F32))
    gap = jnp.minimum(gap, rots - gap)
    bias = prior - 0.5 * norm_img - 0.15 * gap * gap
    bias = jnp.where(valid, bias, LOW)

    flat_bf_ref[...] = flat_ref[...].astype(BF16)
    total = nshift * count
    pairs = [list(range(s, min(s + 4, nshift))) for s in range(0, nshift, 4)]
    peak = None
    build(pairs[0])
    for index, shifts in enumerate(pairs):
        if index + 1 < len(pairs):
            build(pairs[index + 1])
        at = shifts[0] * count
        cross = lax.dot_general(
            flat_bf_ref[...], copies_ref[at : at + len(shifts) * count, :], (((1,), (1,)), ((), ())),
            preferred_element_type=F32,
        )
        for sub in range(0, len(shifts) * count, count):
            logp = cross[:, sub : sub + count] + bias
            weight_ref[:, at + sub : at + sub + count] = logp
            top = jnp.max(logp, axis=0, keepdims=True)
            peak = top if peak is None else jnp.maximum(peak, top)
    mass = jnp.zeros((rpad, count), F32)
    for at in range(0, total, count):
        value = jnp.exp(weight_ref[:, at : at + count] - peak)
        weight_ref[:, at : at + count] = value
        mass = mass + value
    stats_ref[0:1, :] = peak
    stats_ref[1:2, :] = jnp.sum(mass, axis=0, keepdims=True)

    width = share_ref.shape[1]
    if width % 128 == 0:
        start = pl.multiple_of(lax.rem(lax.axis_index("dom") * width, fpix), width)
        share_ctf = ctf_ref[:, pl.ds(start, width)]
        share_ref[...] = share_ctf * share_ctf * inv_ref[:, pl.ds(start, width)]


def estep(images, refs, ctf, inv_noise, log_prior, shifts, rot_prior, groups, rpad, width):
    count, two_f = images.shape
    ngroup, fpix = ctf.shape
    nshift = shifts.shape[0]
    refs = jnp.swapaxes(refs, 0, 1)
    shifts = shifts.T
    return pl.pallas_call(
        estep_kernel,
        out_shape=(
            jax.ShapeDtypeStruct((rpad, nshift * count), F32),
            jax.ShapeDtypeStruct((nshift * count, two_f), BF16),
            jax.ShapeDtypeStruct((2, count), F32),
            jax.ShapeDtypeStruct((ngroup, count), F32),
            jax.ShapeDtypeStruct((ngroup, width), F32),
        ),
        in_specs=[HBM] * 8,
        out_specs=(VMEM,) * 5,
        scratch_shapes=[
            pltpu.VMEM(images.shape, images.dtype),
            pltpu.VMEM(refs.shape, refs.dtype),
            pltpu.VMEM(ctf.shape, F32),
            pltpu.VMEM(ctf.shape, F32),
            pltpu.VMEM(log_prior.shape, F32),
            pltpu.SMEM(shifts.shape, jnp.int32),
            pltpu.VMEM(rot_prior.shape, jnp.int32),
            pltpu.VMEM(groups.shape, jnp.int32),
            pltpu.VMEM((rpad, two_f), F32),
            pltpu.VMEM((rpad, two_f), BF16),
            pltpu.VMEM((count, fpix), F32),
            pltpu.VMEM((round_up(nshift, 8), fpix), F32),
            pltpu.VMEM((round_up(nshift, 8), fpix), F32),
            pltpu.SemaphoreType.DMA((8,)),
        ],
        compiler_params=PARAMS,
        name="estep",
    )(
        *(
            pltpu.with_memory_space_constraint(value, pltpu.HBM)
            for value in (images, refs, ctf, inv_noise, log_prior, shifts, rot_prior, groups)
        )
    )


def posterior(stats_refs, weight_ref, onehot_ref, post_ref, loglik_ref):
    count = onehot_ref.shape[1]
    parts = len(stats_refs)
    me = lax.axis_index("cls")
    stats = [ref[...] for ref in stats_refs]
    ordered = []
    for place in range(parts):
        value = stats[0]
        for ahead in range(1, parts):
            value = jnp.where(me ^ ahead == place, stats[ahead], value)
        ordered.append(value)
    peak = ordered[0][0:1]
    for value in ordered[1:]:
        peak = jnp.maximum(peak, value[0:1])
    total = jnp.zeros_like(peak)
    for value in ordered:
        total = total + value[1:2] * jnp.exp(value[0:1] - peak)
    loglik = peak + jnp.log(total)
    scale = jnp.exp(stats[0][0:1] - loglik)
    loglik_ref[...] = loglik.reshape(count)
    per_img = None
    for at in range(0, weight_ref.shape[1], count):
        post = (weight_ref[:, at : at + count] * scale).astype(BF16)
        post_ref[:, at : at + count] = post
        post = post.astype(F32)
        per_img = post if per_img is None else per_img + post
    three = jnp.concatenate([onehot_ref[...]] * 3, axis=1).astype(BF16)
    hpad = per_img.shape[0] // 2
    return [
        lax.dot_general(
            three, thirds(per_img[at : at + hpad], 1), (((1,), (1,)), ((), ())),
            preferred_element_type=F32,
        )
        for at in (0, hpad)
    ]


def class_sums(post_ref, copies_ref, rows, at, width):
    return jnp.dot(post_ref[rows, :], copies_ref[:, pl.ds(at, width)], preferred_element_type=F32)


LINE = 4
PAIR = 2
SLOW = 4_000_000_000
QUICK = 1000


def owner_column(place, mine, width):
    me = lax.axis_index("dom")
    z = me // PAIR
    y = me % PAIR
    low = z < 2
    stop = [
        jnp.where(low, 3, 0), jnp.where(low, 2, 1), jnp.where(low, 1 - z, 5 - z), z
    ][place]
    side = y if mine else 1 - y
    return pl.multiple_of((stop * PAIR + side) * width, width)


def put_mass(ref, mass):
    ngroup, hpad = mass.shape
    at = ref.shape[0] - ngroup
    ref[at:, 0:hpad] = mass
    ref[at:, hpad:] = jnp.zeros((ngroup, ref.shape[1] - hpad), F32)


def first_kernel(nstat, *refs):
    stats_refs = refs[:nstat]
    weight_ref, copies_ref, onehot_ref, post_ref, send_ref, mass_ref, loglik_ref = refs[nstat:]
    hpad = post_ref.shape[0] // 2
    ngroup = onehot_ref.shape[0]
    width = send_ref.shape[1]
    send = send_ref.shape[0] - ngroup
    mass = posterior(stats_refs, weight_ref, onehot_ref, post_ref, loglik_ref)
    sums = class_sums(post_ref, copies_ref, pl.ds(0, hpad), owner_column(0, False, width), width)
    send_ref[0:send, :] = sums[0:send]
    put_mass(send_ref, mass[0])
    put_mass(mass_ref, mass[1])


def second_kernel(post_ref, copies_ref, mass_ref, send_ref):
    hpad = post_ref.shape[0] // 2
    width = send_ref.shape[1]
    send = send_ref.shape[0] - mass_ref.shape[0]
    sums = class_sums(post_ref, copies_ref, pl.ds(hpad, hpad), owner_column(0, False, width), width)
    send_ref[0:send, :] = sums[0:send]
    send_ref[send:, :] = mass_ref[...]


def rest_kernel(post_ref, copies_ref, send_a_ref, mass_ref, *out_refs):
    hpad = post_ref.shape[0] // 2
    width = mass_ref.shape[1]
    chains = (out_refs[:6], out_refs[6:12])
    send = chains[0][1].shape[0]
    for place in (1, 0, 2, 3):
        for mine in (False, True):
            if place == 0 and not mine:
                continue
            at = owner_column(place, mine, width)

            @pl.when(at >= 0)
            def _(at=at, place=place, mine=mine):
                sums = class_sums(post_ref, copies_ref, pl.ds(0, 2 * hpad), at, width)
                for index, refs in enumerate(chains):
                    value = sums[index * hpad : index * hpad + send]
                    if place == 3 and not mine:
                        out_refs[12][index * send : (index + 1) * send, :] = value
                    else:
                        slot = (0, 1 + int(mine), 3 + int(mine), 5)[place]
                        refs[slot][0:send, :] = value

    chains[0][0][send:, :] = send_a_ref[send:, :]
    chains[1][0][send:, :] = mass_ref[...]


def last_kernel(chain, classes, rots, images, *refs):
    (keep_ref, pair_ref, own_ref, line_ref, cross_ref, share_ref), refs = refs[:6], refs[6:]
    before, refs = (refs[:2], refs[2:]) if chain else (None, refs)
    new_ref, frac_ref, ratio_ref = refs
    send, width = keep_ref.shape
    mine = rots // 2
    z = lax.axis_index("dom") // PAIR
    end = (z == 0) | (z == LINE - 1)
    mass = jnp.where(end, line_ref[send:, :], own_ref[send:, :])
    den = lax.dot_general(
        mass, share_ref[...], (((0,), (0,)), ((), ())), precision=HI, preferred_element_type=F32
    )
    num = keep_ref[...] + pair_ref[chain * send : (chain + 1) * send, :] + line_ref[0:send, :]
    num = num + jnp.where(end, 0.0, cross_ref[...])
    ratio_ref[0:send, :] = num / (den[0:send] + 1.0)
    ratio_ref[send:, :] = jnp.zeros((ratio_ref.shape[0] - send, width), F32)

    piece = 32
    per = 128 // piece
    kpad = round_up(classes, 8)
    lane = lax.broadcasted_iota(jnp.int32, (kpad, 128), 1)
    tiles = []
    values = [
        [ratio_ref[r * classes : r * classes + kpad, base : base + 128] for r in range(mine)]
        for base in range(0, width, 128)
    ]
    for chunk in range(0, width, piece):
        base = chunk // 128 * 128
        parts = []
        for r0 in range(0, mine, per):
            acc = jnp.zeros((kpad, 128), F32)
            for u in range(min(per, mine - r0)):
                turned = values[base // 128][r0 + u]
                turn = (u * piece - (chunk - base)) % 128
                if turn:
                    turned = pltpu.roll(turned, turn, 1)
                acc = jnp.where((lane >= u * piece) & (lane < (u + 1) * piece), turned, acc)
            parts.append(acc)
        tiles.append(jnp.concatenate(parts, axis=1))
    wide = piece * rots
    deep = tiles[0].shape[1]
    src = lax.broadcasted_iota(jnp.int32, (deep, wide), 0)
    dst = lax.broadcasted_iota(jnp.int32, (deep, wide), 1)
    src_r = src // piece
    perm = ((src - src_r * piece) * rots + src_r + chain * mine == dst) & (src_r < mine)
    moved = jnp.dot(
        thirds(jnp.concatenate(tiles, axis=0), 0), perm.astype(BF16), preferred_element_type=F32
    )
    count = len(tiles) * kpad
    moved = moved[0:count] + moved[count : 2 * count] + moved[2 * count :]
    for index in range(len(tiles)):
        columns = slice(index * wide, (index + 1) * wide)
        value = moved[index * kpad : index * kpad + classes, :]
        new_ref[:, columns] = value + before[0][:, columns] if before else value
    mrow = lax.broadcasted_iota(jnp.int32, (width, classes), 0)
    mcol = lax.broadcasted_iota(jnp.int32, (width, classes), 1)
    place = mrow.astype(F32)
    place = place - classes * jnp.floor((place + 0.5) * (1.0 / classes))
    member = ((place == mcol.astype(F32)) & (mrow < mine * classes)).astype(F32)
    share = jnp.dot(
        jnp.sum(mass, axis=0, keepdims=True), member, precision=HI, preferred_element_type=F32
    )
    if before:
        share = share + before[1][...]
        frac_ref[...] = (share / images).reshape(classes)
    else:
        frac_ref[...] = share


def line_path(stats, weight, copies, onehot, share, classes, rots, images):
    half = classes * rots // 2
    send = round_up(half, 8)
    ngroup, width = share.shape
    dom_n = lax.axis_size("dom")
    cls_n = lax.axis_size("cls")
    full = jax.ShapeDtypeStruct((send + ngroup, width), F32)
    body = jax.ShapeDtypeStruct((send, width), F32)
    mass_shape = jax.ShapeDtypeStruct((ngroup, width), F32)

    def first(*refs):
        first_kernel(len(stats), *refs)

    post, send_a, mass_b, loglik = pl.pallas_call(
        first,
        out_shape=(
            jax.ShapeDtypeStruct(weight.shape, BF16),
            full,
            mass_shape,
            jax.ShapeDtypeStruct(onehot.shape[1:], F32),
        ),
        in_specs=[VMEM] * (len(stats) + 3),
        out_specs=(VMEM,) * 4,
        compiler_params=PARAMS,
        name="first_sums",
    )(*stats, weight, copies, onehot)
    send_b = pl.pallas_call(
        second_kernel,
        out_shape=full,
        in_specs=[VMEM] * 3,
        out_specs=VMEM,
        compiler_params=PARAMS,
        name="second_sums",
    )(post, copies, mass_b)
    parts = pl.pallas_call(
        rest_kernel,
        out_shape=((full,) + (body,) * 5) * 2 + (jax.ShapeDtypeStruct((2 * send, width), F32),),
        in_specs=[VMEM] * 4,
        out_specs=(VMEM,) * 13,
        compiler_params=PARAMS,
        name="rest_sums",
    )(post, copies, send_a, mass_b)

    def along(pairs):
        return [(a * PAIR + y, b * PAIR + y) for a, b in pairs for y in range(PAIR)]

    across = [(d, d ^ 1) for d in range(dom_n)]
    outer = along([(0, 1), (1, 0), (2, 3), (3, 2)])
    facing = {0: 0, 1: 2, 2: 1, 3: 3}
    middle = [
        (
            (a * PAIR + y) * cls_n + c,
            (b * PAIR + y) * cls_n + (c if a != b else c ^ 1),
        )
        for a, b in facing.items()
        for y in range(PAIR)
        for c in range(cls_n)
    ]

    def swap(value):
        return lax.ppermute(value, "dom", across)

    def join(kernel, cost, out_shape, *values):
        return pl.pallas_call(
            kernel,
            out_shape=out_shape,
            in_specs=[VMEM] * len(values),
            out_specs=(VMEM,) * len(out_shape),
            compiler_params=PARAMS,
            cost_estimate=pl.CostEstimate(flops=cost, bytes_accessed=0, transcendentals=0),
            name="join",
        )(*values)

    def add2(left, right, out):
        out[...] = left[...] + right[...]

    def join1(keep1, pair1, sum0, got0, sum1, both0):
        sum1[...] = keep1[...] + pair1[...]
        both0[...] = sum0[...] + got0[...]

    def join2(keep2, pair2, sum1, got1, both0, got2, to_ends, to_middle):
        to_middle[...] = sum1[...] + got1[...]
        z = lax.axis_index("dom") // PAIR
        inner = (z != 0) & (z != LINE - 1)
        more = jnp.where(inner, got2[...], 0.0)
        to_ends[0:send, :] = keep2[...] + pair2[...] + more[0:send]
        to_ends[send:, :] = both0[send:, :] + more[send:]


    def reduce_chain(send0, keep0, send1, keep1, send2, keep2):
        pair0 = swap(send0)
        (sum0,) = join(add2, QUICK, (full,), keep0, pair0)
        send1, sum0 = lax.optimization_barrier((send1, sum0))
        pair1 = swap(send1)
        got0 = lax.ppermute(sum0, "dom", outer)
        sum1, both0 = join(join1, SLOW, (body, full), keep1, pair1, sum0, got0)
        send2, sum1, both0 = lax.optimization_barrier((send2, sum1, both0))
        pair2 = swap(send2)
        got1 = lax.ppermute(sum1, "dom", outer)
        got2 = lax.ppermute(both0, ("dom", "cls"), middle)
        to_ends, to_middle = join(
            join2, SLOW, (full, body), keep2, pair2, sum1, got1, both0, got2
        )
        line = lax.ppermute(to_ends, "dom", outer)
        cross = lax.ppermute(to_middle, ("dom", "cls"), middle)
        return pair2, to_ends, line, cross

    chain_a = reduce_chain(send_a, *parts[:5])
    chain_b = reduce_chain(send_b, *parts[6:11])
    send3, _ = lax.optimization_barrier((parts[12], chain_a[0]))
    pair3 = swap(send3)
    pieces_a = (parts[5], pair3) + chain_a[1:]
    pieces_b = (parts[11], pair3) + chain_b[1:]
    before = ()
    for chain, pieces in enumerate((pieces_a, pieces_b)):

        def last(*refs, chain=chain):
            last_kernel(chain, classes, rots, images, *refs)

        before = pl.pallas_call(
            last,
            out_shape=(
                jax.ShapeDtypeStruct((classes, width * rots), F32),
                jax.ShapeDtypeStruct((classes,) if chain else (1, classes), F32),
            ),
            in_specs=[VMEM] * (6 + len(before)),
            out_specs=(VMEM, VMEM),
            scratch_shapes=[pltpu.VMEM((send + 16, width), F32)],
            compiler_params=PARAMS,
            cost_estimate=pl.CostEstimate(flops=QUICK, bytes_accessed=0, transcendentals=0),
            name="last_ratio",
        )(*pieces, share, *before)
    return before[0], loglik, before[1]


def plain_path(stats, weight, copies, onehot, ctf, inv_noise, classes, rots, images):
    rpad = weight.shape[0]
    hpad = rpad // 2
    half = classes * rots // 2
    ngroup, fpix = ctf.shape
    two_f = 2 * fpix
    dom_n = lax.axis_size("dom")
    width = two_f // dom_n
    nstat = len(stats)

    def sums(*refs):
        weight_ref, copies_ref, onehot_ref, num_ref, mass_ref, loglik_ref, post_ref = refs[nstat:]
        mass = posterior(refs[:nstat], weight_ref, onehot_ref, post_ref, loglik_ref)
        mass_ref[0] = mass[0]
        mass_ref[1] = mass[1]
        for at in range(0, two_f, 256):
            num_ref[:, at : at + 256] = class_sums(
                post_ref, copies_ref, pl.ds(0, rpad), at, 256
            )

    num, mass, loglik = pl.pallas_call(
        sums,
        out_shape=(
            jax.ShapeDtypeStruct((rpad, two_f), F32),
            jax.ShapeDtypeStruct((2, ngroup, hpad), F32),
            jax.ShapeDtypeStruct(onehot.shape[1:], F32),
        ),
        in_specs=[VMEM] * (len(stats) + 3),
        out_specs=(VMEM,) * 3,
        scratch_shapes=[pltpu.VMEM(weight.shape, BF16)],
        compiler_params=PARAMS,
        name="all_sums",
    )(*stats, weight, copies, onehot)
    mass = jnp.concatenate([mass[0, :, :half], mass[1, :, :half]], axis=1)
    mass = lax.psum(mass, "dom")
    num = jnp.concatenate([num[:half], num[hpad : hpad + half]], axis=0)
    num = lax.psum_scatter(num, "dom", scatter_dimension=1, tiled=True)
    c2w = ctf * ctf * inv_noise
    c2w_two = jnp.concatenate([c2w, c2w], axis=1)
    c2w_part = lax.dynamic_slice_in_dim(c2w_two, lax.axis_index("dom") * width, width, 1)
    den = jnp.einsum("gn,gq->nq", mass, c2w_part, precision=HI)
    ratio = (num / (den + 1.0)).reshape(rots, classes, width)
    new_refs = ratio.transpose(1, 2, 0).reshape(classes, width * rots)
    frac = jnp.sum(mass.reshape(ngroup, rots, classes), axis=(0, 1)) / images
    return new_refs, loglik, frac


def local(images, refs, ctf, inv_noise, log_prior, shifts, rot_prior, groups):
    classes, rots, two_f = refs.shape
    half = classes * rots // 2
    hpad = round_up(half, 16)
    count = images.shape[0]
    ngroup = ctf.shape[0]
    dom_n = lax.axis_size("dom")
    cls_n = lax.axis_size("cls")
    width = two_f // dom_n
    weight, copies, stat, onehot, share = estep(
        images, refs, ctf, inv_noise, log_prior, shifts, rot_prior, groups, 2 * hpad, width
    )
    if cls_n & (cls_n - 1):
        raise ValueError("cls size")
    stats = [stat] + [
        lax.ppermute(stat, "cls", [(c, c ^ other) for c in range(cls_n)])
        for other in range(1, cls_n)
    ]
    fits = (
        dom_n == LINE * PAIR
        and cls_n % 2 == 0
        and width % 128 == 0
        and hpad <= width
        and ngroup % 8 == 0
    )
    images_n = count * dom_n
    if fits:
        return line_path(stats, weight, copies, onehot, share, classes, rots, images_n)
    return plain_path(stats, weight, copies, onehot, ctf, inv_noise, classes, rots, images_n)


def solution(mesh):
    return jax.shard_map(
        local,
        mesh=mesh,
        in_specs=(
            P("dom", None),
            P("cls", None, None),
            P(),
            P(),
            P("cls"),
            P(),
            P("dom"),
            P("dom"),
        ),
        out_specs=(P("cls", "dom"), P("dom"), P("cls")),
        check_vma=False,
    )
```

```python
import math

import jax
import jax.numpy as jnp
from jax import lax
from jax.experimental import pallas as pl
from jax.experimental.pallas import tpu as pltpu
from jax.sharding import PartitionSpec as P

HI = lax.Precision.HIGHEST
F32 = jnp.float32
BF16 = jnp.bfloat16
VMEM = pl.BlockSpec(memory_space=pltpu.VMEM)
HBM = pl.BlockSpec(memory_space=pltpu.HBM)
PARAMS = pltpu.CompilerParams(vmem_limit_bytes=20 * 1024 * 1024)
LOW = -1e30


def round_up(value, multiple):
    return -(-value // multiple) * multiple


def split(value):
    high = value.astype(BF16)
    rest = value - high.astype(F32)
    middle = rest.astype(BF16)
    return high, middle, (rest - middle.astype(F32)).astype(BF16)


def thirds(value, axis):
    return jnp.concatenate(split(value), axis=axis)


def estep_kernel(
    images_hbm, refs_hbm, ctf_hbm, inv_hbm, prior_hbm, shifts_hbm, rot_hbm, groups_hbm,
    weight_ref, copies_ref, stats_ref, onehot_ref, share_ref,
    images_ref, refs_ref, ctf_ref, inv_ref, prior_ref, shifts_ref, rot_ref, groups_ref,
    flat_ref, flat_bf_ref, cw_ref, cos_ref, sin_ref, sems,
):
    count, two_f = images_ref.shape
    fpix = two_f // 2
    rots, classes, _ = refs_ref.shape
    ngroup = ctf_ref.shape[0]
    nshift = shifts_ref.shape[1]
    rpad = flat_ref.shape[0]
    half = classes * rots // 2
    hpad = rpad // 2

    loads = [
        pltpu.make_async_copy(src, dst, sems.at[index])
        for index, (src, dst) in enumerate(
            (
                (shifts_hbm, shifts_ref),
                (groups_hbm, groups_ref),
                (ctf_hbm, ctf_ref),
                (inv_hbm, inv_ref),
                (images_hbm, images_ref),
                (refs_hbm, refs_ref),
                (prior_hbm, prior_ref),
                (rot_hbm, rot_ref),
            )
        )
    ]
    for load in loads:
        load.start()
    side = int(math.isqrt(fpix))
    pos = lax.broadcasted_iota(jnp.int32, (1, fpix), 1).astype(F32)
    line = jnp.floor((pos + 0.5) * (1.0 / side))
    freq_x = pos - side * line
    freq_y = line - side // 2
    loads[0].wait()
    index = lax.broadcasted_iota(jnp.int32, (cos_ref.shape[0], 1), 0)
    shift_x = jnp.zeros(index.shape, F32)
    shift_y = jnp.zeros(index.shape, F32)
    for s in range(nshift):
        shift_x = jnp.where(index == s, shifts_ref[0, s].astype(F32), shift_x)
        shift_y = jnp.where(index == s, shifts_ref[1, s].astype(F32), shift_y)
    angle = 2.0 * math.pi * (shift_x * freq_x + shift_y * freq_y) / 256.0
    cos_ref[...] = jnp.cos(angle)
    sin_ref[...] = jnp.sin(angle)

    for load in loads[1:4]:
        load.wait()
    own = groups_ref[...].reshape(1, count)
    onehot = (own == lax.broadcasted_iota(jnp.int32, (ngroup, count), 0)).astype(F32)
    onehot_ref[...] = onehot
    three = jnp.concatenate([onehot] * 3, axis=0).astype(BF16)
    weight = ctf_ref[...] * inv_ref[...]
    cw_ref[...] = lax.dot_general(
        three, thirds(weight, 0), (((0,), (0,)), ((), ())), preferred_element_type=F32
    )
    loads[4].wait()

    def build(shifts):
        for at in range(0, count, 16):
            for lane in range(0, fpix, 128):
                cw = cw_ref[at : at + 16, lane : lane + 128]
                real = images_ref[at : at + 16, lane : lane + 128].astype(F32) * cw
                imag = images_ref[at : at + 16, fpix + lane : fpix + lane + 128].astype(F32) * cw
                for s in shifts:
                    c = cos_ref[s : s + 1, lane : lane + 128]
                    d = sin_ref[s : s + 1, lane : lane + 128]
                    to = s * count + at
                    copies_ref[to : to + 16, lane : lane + 128] = (real * c + imag * d).astype(BF16)
                    copies_ref[to : to + 16, fpix + lane : fpix + lane + 128] = (
                        imag * c - real * d
                    ).astype(BF16)

    for load in loads[5:]:
        load.wait()
    for side in range(2):
        flat_ref[side * hpad + half : (side + 1) * hpad, :] = jnp.zeros((hpad - half, two_f), F32)
        for r in range(rots // 2):
            at = side * hpad + r * classes
            flat_ref[at : at + classes, :] = refs_ref[side * (rots // 2) + r].astype(F32)
    power = flat_ref[:, :fpix] ** 2 + flat_ref[:, fpix:] ** 2
    c2w = ctf_ref[...] * ctf_ref[...] * inv_ref[...]
    high = power.astype(BF16)
    low = (power - high.astype(F32)).astype(BF16)
    c2w = thirds(c2w, 0)
    norms = lax.dot_general(
        c2w, high, (((1,), (1,)), ((), ())), preferred_element_type=F32
    ) + lax.dot_general(c2w, low, (((1,), (1,)), ((), ())), preferred_element_type=F32)
    norms = norms[:ngroup] + norms[ngroup : 2 * ngroup] + norms[2 * ngroup :]
    norm_img = lax.dot_general(
        thirds(norms, 0), three, (((0,), (0,)), ((), ())), preferred_element_type=F32
    )
    row = lax.broadcasted_iota(jnp.int32, (rpad, 1), 0)
    row = jnp.where(row < hpad, row, row - hpad + half)
    valid = (row < half) | ((row >= half) & (lax.broadcasted_iota(jnp.int32, (rpad, 1), 0) >= hpad))
    valid = valid & (row < 2 * half)
    row = row.astype(F32)
    rot = jnp.floor((row + 0.5) * (1.0 / classes))
    lane = lax.broadcasted_iota(jnp.int32, (rpad, classes), 1).astype(F32)
    own = jnp.where(lane == row - rot * classes, prior_ref[...].reshape(1, classes), 0.0)
    prior = jnp.sum(own, axis=1, keepdims=True)
    gap = jnp.abs(rot - rot_ref[...].reshape(1, count).astype(F32))
    gap = jnp.minimum(gap, rots - gap)
    bias = prior - 0.5 * norm_img - 0.15 * gap * gap
    bias = jnp.where(valid, bias, LOW)

    flat_bf_ref[...] = flat_ref[...].astype(BF16)
    total = nshift * count
    pairs = [list(range(s, min(s + 4, nshift))) for s in range(0, nshift, 4)]
    peak = None
    build(pairs[0])
    for index, shifts in enumerate(pairs):
        if index + 1 < len(pairs):
            build(pairs[index + 1])
        at = shifts[0] * count
        cross = lax.dot_general(
            flat_bf_ref[...], copies_ref[at : at + len(shifts) * count, :], (((1,), (1,)), ((), ())),
            preferred_element_type=F32,
        )
        for sub in range(0, len(shifts) * count, count):
            logp = cross[:, sub : sub + count] + bias
            weight_ref[:, at + sub : at + sub + count] = logp
            top = jnp.max(logp, axis=0, keepdims=True)
            peak = top if peak is None else jnp.maximum(peak, top)
    mass = jnp.zeros((rpad, count), F32)
    for at in range(0, total, count):
        value = jnp.exp(weight_ref[:, at : at + count] - peak)
        weight_ref[:, at : at + count] = value
        mass = mass + value
    stats_ref[0:1, :] = peak
    stats_ref[1:2, :] = jnp.sum(mass, axis=0, keepdims=True)

    width = share_ref.shape[1]
    if width % 128 == 0:
        start = pl.multiple_of(lax.rem(lax.axis_index("dom") * width, fpix), width)
        share_ctf = ctf_ref[:, pl.ds(start, width)]
        share_ref[...] = share_ctf * share_ctf * inv_ref[:, pl.ds(start, width)]


def estep(images, refs, ctf, inv_noise, log_prior, shifts, rot_prior, groups, rpad, width):
    count, two_f = images.shape
    ngroup, fpix = ctf.shape
    nshift = shifts.shape[0]
    refs = jnp.swapaxes(refs, 0, 1)
    shifts = shifts.T
    return pl.pallas_call(
        estep_kernel,
        out_shape=(
            jax.ShapeDtypeStruct((rpad, nshift * count), F32),
            jax.ShapeDtypeStruct((nshift * count, two_f), BF16),
            jax.ShapeDtypeStruct((2, count), F32),
            jax.ShapeDtypeStruct((ngroup, count), F32),
            jax.ShapeDtypeStruct((ngroup, width), F32),
        ),
        in_specs=[HBM] * 8,
        out_specs=(VMEM,) * 5,
        scratch_shapes=[
            pltpu.VMEM(images.shape, images.dtype),
            pltpu.VMEM(refs.shape, refs.dtype),
            pltpu.VMEM(ctf.shape, F32),
            pltpu.VMEM(ctf.shape, F32),
            pltpu.VMEM(log_prior.shape, F32),
            pltpu.SMEM(shifts.shape, jnp.int32),
            pltpu.VMEM(rot_prior.shape, jnp.int32),
            pltpu.VMEM(groups.shape, jnp.int32),
            pltpu.VMEM((rpad, two_f), F32),
            pltpu.VMEM((rpad, two_f), BF16),
            pltpu.VMEM((count, fpix), F32),
            pltpu.VMEM((round_up(nshift, 8), fpix), F32),
            pltpu.VMEM((round_up(nshift, 8), fpix), F32),
            pltpu.SemaphoreType.DMA((8,)),
        ],
        compiler_params=PARAMS,
        name="estep",
    )(
        *(
            pltpu.with_memory_space_constraint(value, pltpu.HBM)
            for value in (images, refs, ctf, inv_noise, log_prior, shifts, rot_prior, groups)
        )
    )


def posterior(stats_refs, weight_ref, onehot_ref, post_ref, loglik_ref):
    count = onehot_ref.shape[1]
    parts = len(stats_refs)
    me = lax.axis_index("cls")
    stats = [ref[...] for ref in stats_refs]
    ordered = []
    for place in range(parts):
        value = stats[0]
        for ahead in range(1, parts):
            value = jnp.where(me ^ ahead == place, stats[ahead], value)
        ordered.append(value)
    peak = ordered[0][0:1]
    for value in ordered[1:]:
        peak = jnp.maximum(peak, value[0:1])
    total = jnp.zeros_like(peak)
    for value in ordered:
        total = total + value[1:2] * jnp.exp(value[0:1] - peak)
    loglik = peak + jnp.log(total)
    scale = jnp.exp(stats[0][0:1] - loglik)
    loglik_ref[...] = loglik.reshape(count)
    per_img = None
    for at in range(0, weight_ref.shape[1], count):
        post = (weight_ref[:, at : at + count] * scale).astype(BF16)
        post_ref[:, at : at + count] = post
        post = post.astype(F32)
        per_img = post if per_img is None else per_img + post
    three = jnp.concatenate([onehot_ref[...]] * 3, axis=1).astype(BF16)
    hpad = per_img.shape[0] // 2
    return [
        lax.dot_general(
            three, thirds(per_img[at : at + hpad], 1), (((1,), (1,)), ((), ())),
            preferred_element_type=F32,
        )
        for at in (0, hpad)
    ]


def class_sums(post_ref, copies_ref, rows, at, width):
    return jnp.dot(post_ref[rows, :], copies_ref[:, pl.ds(at, width)], preferred_element_type=F32)


LINE = 4
PAIR = 2
SLOW = 4_000_000_000
QUICK = 1000


def owner_column(place, mine, width):
    me = lax.axis_index("dom")
    z = me // PAIR
    y = me % PAIR
    low = z < 2
    stop = [
        jnp.where(low, 3, 0), jnp.where(low, 2, 1), jnp.where(low, 1 - z, 5 - z), z
    ][place]
    side = y if mine else 1 - y
    return pl.multiple_of((stop * PAIR + side) * width, width)


def put_mass(ref, mass):
    ngroup, hpad = mass.shape
    at = ref.shape[0] - ngroup
    ref[at:, 0:hpad] = mass
    ref[at:, hpad:] = jnp.zeros((ngroup, ref.shape[1] - hpad), F32)


def first_kernel(nstat, *refs):
    stats_refs = refs[:nstat]
    weight_ref, copies_ref, onehot_ref, post_ref, send_ref, mass_ref, loglik_ref = refs[nstat:]
    hpad = post_ref.shape[0] // 2
    ngroup = onehot_ref.shape[0]
    width = send_ref.shape[1]
    send = send_ref.shape[0] - ngroup
    mass = posterior(stats_refs, weight_ref, onehot_ref, post_ref, loglik_ref)
    sums = class_sums(post_ref, copies_ref, pl.ds(0, hpad), owner_column(0, False, width), width)
    send_ref[0:send, :] = sums[0:send]
    put_mass(send_ref, mass[0])
    put_mass(mass_ref, mass[1])


def second_kernel(post_ref, copies_ref, mass_ref, send_ref):
    hpad = post_ref.shape[0] // 2
    width = send_ref.shape[1]
    send = send_ref.shape[0] - mass_ref.shape[0]
    sums = class_sums(post_ref, copies_ref, pl.ds(hpad, hpad), owner_column(0, False, width), width)
    send_ref[0:send, :] = sums[0:send]
    send_ref[send:, :] = mass_ref[...]


def rest_kernel(post_ref, copies_ref, send_a_ref, mass_ref, *out_refs):
    hpad = post_ref.shape[0] // 2
    width = mass_ref.shape[1]
    chains = (out_refs[:6], out_refs[6:12])
    send = chains[0][1].shape[0]
    for place in (1, 0, 2, 3):
        for mine in (False, True):
            if place == 0 and not mine:
                continue
            at = owner_column(place, mine, width)

            @pl.when(at >= 0)
            def _(at=at, place=place, mine=mine):
                sums = class_sums(post_ref, copies_ref, pl.ds(0, 2 * hpad), at, width)
                for index, refs in enumerate(chains):
                    value = sums[index * hpad : index * hpad + send]
                    if place == 3 and not mine:
                        out_refs[12][index * send : (index + 1) * send, :] = value
                    else:
                        slot = (0, 1 + int(mine), 3 + int(mine), 5)[place]
                        refs[slot][0:send, :] = value

    chains[0][0][send:, :] = send_a_ref[send:, :]
    chains[1][0][send:, :] = mass_ref[...]


def last_kernel(chain, classes, rots, images, *refs):
    (keep_ref, pair_ref, own_ref, line_ref, cross_ref, share_ref), refs = refs[:6], refs[6:]
    before, refs = (refs[:2], refs[2:]) if chain else (None, refs)
    new_ref, frac_ref, ratio_ref = refs
    send, width = keep_ref.shape
    mine = rots // 2
    z = lax.axis_index("dom") // PAIR
    end = (z == 0) | (z == LINE - 1)
    mass = jnp.where(end, line_ref[send:, :], own_ref[send:, :])
    mass_high, mass_middle, mass_low = split(mass)
    high, middle, low = split(share_ref[...])
    den = lax.dot_general(
        jnp.concatenate([mass_high] * 3 + [mass_middle] * 2 + [mass_low], axis=0),
        jnp.concatenate([high, middle, low, high, middle, high], axis=0),
        (((0,), (0,)), ((), ())),
        preferred_element_type=F32,
    )
    num = keep_ref[...] + pair_ref[chain * send : (chain + 1) * send, :] + line_ref[0:send, :]
    num = num + jnp.where(end, 0.0, cross_ref[...])
    ratio_ref[0:send, :] = num / (den[0:send] + 1.0)
    ratio_ref[send:, :] = jnp.zeros((ratio_ref.shape[0] - send, width), F32)

    piece = 32
    per = 128 // piece
    kpad = round_up(classes, 8)
    lane = lax.broadcasted_iota(jnp.int32, (kpad, 128), 1)
    tiles = []
    values = [
        [ratio_ref[r * classes : r * classes + kpad, base : base + 128] for r in range(mine)]
        for base in range(0, width, 128)
    ]
    for chunk in range(0, width, piece):
        base = chunk // 128 * 128
        parts = []
        for r0 in range(0, mine, per):
            acc = jnp.zeros((kpad, 128), F32)
            for u in range(min(per, mine - r0)):
                turned = values[base // 128][r0 + u]
                turn = (u * piece - (chunk - base)) % 128
                if turn:
                    turned = pltpu.roll(turned, turn, 1)
                acc = jnp.where((lane >= u * piece) & (lane < (u + 1) * piece), turned, acc)
            parts.append(acc)
        tiles.append(jnp.concatenate(parts, axis=1))
    wide = piece * rots
    deep = tiles[0].shape[1]
    src = lax.broadcasted_iota(jnp.int32, (deep, wide), 0)
    dst = lax.broadcasted_iota(jnp.int32, (deep, wide), 1)
    src_r = src // piece
    perm = ((src - src_r * piece) * rots + src_r + chain * mine == dst) & (src_r < mine)
    moved = jnp.dot(
        thirds(jnp.concatenate(tiles, axis=0), 0), perm.astype(BF16), preferred_element_type=F32
    )
    count = len(tiles) * kpad
    moved = moved[0:count] + moved[count : 2 * count] + moved[2 * count :]
    for index in range(len(tiles)):
        columns = slice(index * wide, (index + 1) * wide)
        value = moved[index * kpad : index * kpad + classes, :]
        new_ref[:, columns] = value + before[0][:, columns] if before else value
    mrow = lax.broadcasted_iota(jnp.int32, (width, classes), 0)
    mcol = lax.broadcasted_iota(jnp.int32, (width, classes), 1)
    place = mrow.astype(F32)
    place = place - classes * jnp.floor((place + 0.5) * (1.0 / classes))
    member = ((place == mcol.astype(F32)) & (mrow < mine * classes)).astype(F32)
    share = jnp.dot(
        thirds(jnp.sum(mass, axis=0, keepdims=True), 0), member.astype(BF16),
        preferred_element_type=F32,
    )
    share = jnp.sum(share, axis=0, keepdims=True)
    if before:
        share = share + before[1][...]
        frac_ref[...] = (share / images).reshape(classes)
    else:
        frac_ref[...] = share


def line_path(stats, weight, copies, onehot, share, classes, rots, images):
    half = classes * rots // 2
    send = round_up(half, 8)
    ngroup, width = share.shape
    dom_n = lax.axis_size("dom")
    cls_n = lax.axis_size("cls")
    full = jax.ShapeDtypeStruct((send + ngroup, width), F32)
    body = jax.ShapeDtypeStruct((send, width), F32)
    mass_shape = jax.ShapeDtypeStruct((ngroup, width), F32)

    def first(*refs):
        first_kernel(len(stats), *refs)

    post, send_a, mass_b, loglik = pl.pallas_call(
        first,
        out_shape=(
            jax.ShapeDtypeStruct(weight.shape, BF16),
            full,
            mass_shape,
            jax.ShapeDtypeStruct(onehot.shape[1:], F32),
        ),
        in_specs=[VMEM] * (len(stats) + 3),
        out_specs=(VMEM,) * 4,
        compiler_params=PARAMS,
        name="first_sums",
    )(*stats, weight, copies, onehot)
    send_b = pl.pallas_call(
        second_kernel,
        out_shape=full,
        in_specs=[VMEM] * 3,
        out_specs=VMEM,
        compiler_params=PARAMS,
        name="second_sums",
    )(post, copies, mass_b)
    parts = pl.pallas_call(
        rest_kernel,
        out_shape=((full,) + (body,) * 5) * 2 + (jax.ShapeDtypeStruct((2 * send, width), F32),),
        in_specs=[VMEM] * 4,
        out_specs=(VMEM,) * 13,
        compiler_params=PARAMS,
        name="rest_sums",
    )(post, copies, send_a, mass_b)

    def along(pairs):
        return [(a * PAIR + y, b * PAIR + y) for a, b in pairs for y in range(PAIR)]

    across = [(d, d ^ 1) for d in range(dom_n)]
    outer = along([(0, 1), (1, 0), (2, 3), (3, 2)])
    facing = {0: 0, 1: 2, 2: 1, 3: 3}
    middle = [
        (
            (a * PAIR + y) * cls_n + c,
            (b * PAIR + y) * cls_n + (c if a != b else c ^ 1),
        )
        for a, b in facing.items()
        for y in range(PAIR)
        for c in range(cls_n)
    ]

    def swap(value):
        return lax.ppermute(value, "dom", across)

    def join(kernel, cost, out_shape, *values):
        return pl.pallas_call(
            kernel,
            out_shape=out_shape,
            in_specs=[VMEM] * len(values),
            out_specs=(VMEM,) * len(out_shape),
            compiler_params=PARAMS,
            cost_estimate=pl.CostEstimate(flops=cost, bytes_accessed=0, transcendentals=0),
            name="join",
        )(*values)

    def add2(left, right, out):
        out[...] = left[...] + right[...]

    def join1(keep1, pair1, sum0, got0, sum1, both0):
        sum1[...] = keep1[...] + pair1[...]
        both0[...] = sum0[...] + got0[...]

    def join2(keep2, pair2, sum1, got1, both0, got2, to_ends, to_middle):
        to_middle[...] = sum1[...] + got1[...]
        z = lax.axis_index("dom") // PAIR
        inner = (z != 0) & (z != LINE - 1)
        more = jnp.where(inner, got2[...], 0.0)
        to_ends[0:send, :] = keep2[...] + pair2[...] + more[0:send]
        to_ends[send:, :] = both0[send:, :] + more[send:]


    def reduce_chain(send0, keep0, send1, keep1, send2, keep2):
        pair0 = swap(send0)
        (sum0,) = join(add2, QUICK, (full,), keep0, pair0)
        send1, sum0 = lax.optimization_barrier((send1, sum0))
        pair1 = swap(send1)
        got0 = lax.ppermute(sum0, "dom", outer)
        sum1, both0 = join(join1, SLOW, (body, full), keep1, pair1, sum0, got0)
        send2, sum1, both0 = lax.optimization_barrier((send2, sum1, both0))
        pair2 = swap(send2)
        got1 = lax.ppermute(sum1, "dom", outer)
        got2 = lax.ppermute(both0, ("dom", "cls"), middle)
        to_ends, to_middle = join(
            join2, SLOW, (full, body), keep2, pair2, sum1, got1, both0, got2
        )
        line = lax.ppermute(to_ends, "dom", outer)
        cross = lax.ppermute(to_middle, ("dom", "cls"), middle)
        return pair2, to_ends, line, cross

    chain_a = reduce_chain(send_a, *parts[:5])
    chain_b = reduce_chain(send_b, *parts[6:11])
    send3, _ = lax.optimization_barrier((parts[12], chain_a[0]))
    pair3 = swap(send3)
    pieces_a = (parts[5], pair3) + chain_a[1:]
    pieces_b = (parts[11], pair3) + chain_b[1:]
    before = ()
    for chain, pieces in enumerate((pieces_a, pieces_b)):

        def last(*refs, chain=chain):
            last_kernel(chain, classes, rots, images, *refs)

        before = pl.pallas_call(
            last,
            out_shape=(
                jax.ShapeDtypeStruct((classes, width * rots), F32),
                jax.ShapeDtypeStruct((classes,) if chain else (1, classes), F32),
            ),
            in_specs=[VMEM] * (6 + len(before)),
            out_specs=(VMEM, VMEM),
            scratch_shapes=[pltpu.VMEM((send + 16, width), F32)],
            compiler_params=PARAMS,
            cost_estimate=pl.CostEstimate(flops=QUICK, bytes_accessed=0, transcendentals=0),
            name="last_ratio",
        )(*pieces, share, *before)
    return before[0], loglik, before[1]


def plain_path(stats, weight, copies, onehot, ctf, inv_noise, classes, rots, images):
    rpad = weight.shape[0]
    hpad = rpad // 2
    half = classes * rots // 2
    ngroup, fpix = ctf.shape
    two_f = 2 * fpix
    dom_n = lax.axis_size("dom")
    width = two_f // dom_n
    nstat = len(stats)

    def sums(*refs):
        weight_ref, copies_ref, onehot_ref, num_ref, mass_ref, loglik_ref, post_ref = refs[nstat:]
        mass = posterior(refs[:nstat], weight_ref, onehot_ref, post_ref, loglik_ref)
        mass_ref[0] = mass[0]
        mass_ref[1] = mass[1]
        for at in range(0, two_f, 256):
            num_ref[:, at : at + 256] = class_sums(
                post_ref, copies_ref, pl.ds(0, rpad), at, 256
            )

    num, mass, loglik = pl.pallas_call(
        sums,
        out_shape=(
            jax.ShapeDtypeStruct((rpad, two_f), F32),
            jax.ShapeDtypeStruct((2, ngroup, hpad), F32),
            jax.ShapeDtypeStruct(onehot.shape[1:], F32),
        ),
        in_specs=[VMEM] * (len(stats) + 3),
        out_specs=(VMEM,) * 3,
        scratch_shapes=[pltpu.VMEM(weight.shape, BF16)],
        compiler_params=PARAMS,
        name="all_sums",
    )(*stats, weight, copies, onehot)
    mass = jnp.concatenate([mass[0, :, :half], mass[1, :, :half]], axis=1)
    mass = lax.psum(mass, "dom")
    num = jnp.concatenate([num[:half], num[hpad : hpad + half]], axis=0)
    num = lax.psum_scatter(num, "dom", scatter_dimension=1, tiled=True)
    c2w = ctf * ctf * inv_noise
    c2w_two = jnp.concatenate([c2w, c2w], axis=1)
    c2w_part = lax.dynamic_slice_in_dim(c2w_two, lax.axis_index("dom") * width, width, 1)
    den = jnp.einsum("gn,gq->nq", mass, c2w_part, precision=HI)
    ratio = (num / (den + 1.0)).reshape(rots, classes, width)
    new_refs = ratio.transpose(1, 2, 0).reshape(classes, width * rots)
    frac = jnp.sum(mass.reshape(ngroup, rots, classes), axis=(0, 1)) / images
    return new_refs, loglik, frac


def local(images, refs, ctf, inv_noise, log_prior, shifts, rot_prior, groups):
    classes, rots, two_f = refs.shape
    half = classes * rots // 2
    hpad = round_up(half, 16)
    count = images.shape[0]
    ngroup = ctf.shape[0]
    dom_n = lax.axis_size("dom")
    cls_n = lax.axis_size("cls")
    width = two_f // dom_n
    weight, copies, stat, onehot, share = estep(
        images, refs, ctf, inv_noise, log_prior, shifts, rot_prior, groups, 2 * hpad, width
    )
    if cls_n & (cls_n - 1):
        raise ValueError("cls size")
    stats = [stat] + [
        lax.ppermute(stat, "cls", [(c, c ^ other) for c in range(cls_n)])
        for other in range(1, cls_n)
    ]
    fits = (
        dom_n == LINE * PAIR
        and cls_n % 2 == 0
        and width % 128 == 0
        and hpad <= width
        and ngroup % 8 == 0
    )
    images_n = count * dom_n
    if fits:
        return line_path(stats, weight, copies, onehot, share, classes, rots, images_n)
    return plain_path(stats, weight, copies, onehot, ctf, inv_noise, classes, rots, images_n)


def solution(mesh):
    return jax.shard_map(
        local,
        mesh=mesh,
        in_specs=(
            P("dom", None),
            P("cls", None, None),
            P(),
            P(),
            P("cls"),
            P(),
            P("dom"),
            P("dom"),
        ),
        out_specs=(P("cls", "dom"), P("dom"), P("cls")),
        check_vma=False,
    )
```

```python
import math

import jax
import jax.numpy as jnp
from jax import lax
from jax.experimental import pallas as pl
from jax.experimental.pallas import tpu as pltpu
from jax.sharding import PartitionSpec as P

HI = lax.Precision.HIGHEST
F32 = jnp.float32
BF16 = jnp.bfloat16
VMEM = pl.BlockSpec(memory_space=pltpu.VMEM)
HBM = pl.BlockSpec(memory_space=pltpu.HBM)
PARAMS = pltpu.CompilerParams(vmem_limit_bytes=20 * 1024 * 1024)
LOW = -1e30


def round_up(value, multiple):
    return -(-value // multiple) * multiple


def split(value):
    high = value.astype(BF16)
    rest = value - high.astype(F32)
    middle = rest.astype(BF16)
    return high, middle, (rest - middle.astype(F32)).astype(BF16)


def thirds(value, axis):
    return jnp.concatenate(split(value), axis=axis)


def estep_kernel(
    images_hbm, refs_hbm, ctf_hbm, inv_hbm, prior_hbm, shifts_hbm, rot_hbm, groups_hbm,
    weight_ref, copies_ref, stats_ref, onehot_ref, share_ref,
    images_ref, refs_ref, ctf_ref, inv_ref, prior_ref, shifts_ref, rot_ref, groups_ref,
    flat_ref, flat_bf_ref, cw_ref, cos_ref, sin_ref, sems,
):
    count, two_f = images_ref.shape
    fpix = two_f // 2
    rots, classes, _ = refs_ref.shape
    ngroup = ctf_ref.shape[0]
    nshift = shifts_ref.shape[1]
    rpad = flat_ref.shape[0]
    half = classes * rots // 2
    hpad = rpad // 2

    loads = [
        pltpu.make_async_copy(src, dst, sems.at[index])
        for index, (src, dst) in enumerate(
            (
                (shifts_hbm, shifts_ref),
                (groups_hbm, groups_ref),
                (ctf_hbm, ctf_ref),
                (inv_hbm, inv_ref),
                (images_hbm, images_ref),
                (refs_hbm, refs_ref),
                (prior_hbm, prior_ref),
                (rot_hbm, rot_ref),
            )
        )
    ]
    for load in loads:
        load.start()
    side = int(math.isqrt(fpix))
    pos = lax.broadcasted_iota(jnp.int32, (1, fpix), 1).astype(F32)
    line = jnp.floor((pos + 0.5) * (1.0 / side))
    freq_x = pos - side * line
    freq_y = line - side // 2
    loads[0].wait()
    index = lax.broadcasted_iota(jnp.int32, (cos_ref.shape[0], 1), 0)
    shift_x = jnp.zeros(index.shape, F32)
    shift_y = jnp.zeros(index.shape, F32)
    for s in range(nshift):
        shift_x = jnp.where(index == s, shifts_ref[0, s].astype(F32), shift_x)
        shift_y = jnp.where(index == s, shifts_ref[1, s].astype(F32), shift_y)
    angle = 2.0 * math.pi * (shift_x * freq_x + shift_y * freq_y) / 256.0
    cos_ref[...] = jnp.cos(angle)
    sin_ref[...] = jnp.sin(angle)

    for load in loads[1:4]:
        load.wait()
    own = groups_ref[...].reshape(1, count)
    onehot = (own == lax.broadcasted_iota(jnp.int32, (ngroup, count), 0)).astype(F32)
    onehot_ref[...] = onehot
    three = jnp.concatenate([onehot] * 3, axis=0).astype(BF16)
    weight = ctf_ref[...] * inv_ref[...]
    cw_ref[...] = lax.dot_general(
        three, thirds(weight, 0), (((0,), (0,)), ((), ())), preferred_element_type=F32
    )
    loads[4].wait()

    def build(shifts):
        for at in range(0, count, 16):
            for lane in range(0, fpix, 128):
                cw = cw_ref[at : at + 16, lane : lane + 128]
                real = images_ref[at : at + 16, lane : lane + 128].astype(F32) * cw
                imag = images_ref[at : at + 16, fpix + lane : fpix + lane + 128].astype(F32) * cw
                for s in shifts:
                    c = cos_ref[s : s + 1, lane : lane + 128]
                    d = sin_ref[s : s + 1, lane : lane + 128]
                    to = s * count + at
                    copies_ref[to : to + 16, lane : lane + 128] = (real * c + imag * d).astype(BF16)
                    copies_ref[to : to + 16, fpix + lane : fpix + lane + 128] = (
                        imag * c - real * d
                    ).astype(BF16)

    for load in loads[5:]:
        load.wait()
    for side in range(2):
        flat_ref[side * hpad + half : (side + 1) * hpad, :] = jnp.zeros((hpad - half, two_f), F32)
        for r in range(rots // 2):
            at = side * hpad + r * classes
            flat_ref[at : at + classes, :] = refs_ref[side * (rots // 2) + r].astype(F32)
    power = flat_ref[:, :fpix] ** 2 + flat_ref[:, fpix:] ** 2
    c2w = ctf_ref[...] * ctf_ref[...] * inv_ref[...]
    high = power.astype(BF16)
    low = (power - high.astype(F32)).astype(BF16)
    c2w = thirds(c2w, 0)
    norms = lax.dot_general(
        c2w, high, (((1,), (1,)), ((), ())), preferred_element_type=F32
    ) + lax.dot_general(c2w, low, (((1,), (1,)), ((), ())), preferred_element_type=F32)
    norms = norms[:ngroup] + norms[ngroup : 2 * ngroup] + norms[2 * ngroup :]
    norm_img = lax.dot_general(
        thirds(norms, 0), three, (((0,), (0,)), ((), ())), preferred_element_type=F32
    )
    row = lax.broadcasted_iota(jnp.int32, (rpad, 1), 0)
    row = jnp.where(row < hpad, row, row - hpad + half)
    valid = (row < half) | ((row >= half) & (lax.broadcasted_iota(jnp.int32, (rpad, 1), 0) >= hpad))
    valid = valid & (row < 2 * half)
    row = row.astype(F32)
    rot = jnp.floor((row + 0.5) * (1.0 / classes))
    lane = lax.broadcasted_iota(jnp.int32, (rpad, classes), 1).astype(F32)
    own = jnp.where(lane == row - rot * classes, prior_ref[...].reshape(1, classes), 0.0)
    prior = jnp.sum(own, axis=1, keepdims=True)
    gap = jnp.abs(rot - rot_ref[...].reshape(1, count).astype(F32))
    gap = jnp.minimum(gap, rots - gap)
    bias = prior - 0.5 * norm_img - 0.15 * gap * gap
    bias = jnp.where(valid, bias, LOW)

    flat_bf_ref[...] = flat_ref[...].astype(BF16)
    total = nshift * count
    part = -(-nshift // 2)
    parts = [list(range(s, min(s + part, nshift))) for s in range(0, nshift, part)]
    peak = None
    build(parts[0])
    for index, shifts in enumerate(parts):
        if index + 1 < len(parts):
            build(parts[index + 1])
        at = shifts[0] * count
        cross = lax.dot_general(
            flat_bf_ref[...], copies_ref[at : at + len(shifts) * count, :], (((1,), (1,)), ((), ())),
            preferred_element_type=F32,
        )
        for sub in range(0, len(shifts) * count, count):
            logp = cross[:, sub : sub + count] + bias
            weight_ref[:, at + sub : at + sub + count] = logp
            top = jnp.max(logp, axis=0, keepdims=True)
            peak = top if peak is None else jnp.maximum(peak, top)
    mass = jnp.zeros((rpad, count), F32)
    for at in range(0, total, count):
        value = jnp.exp(weight_ref[:, at : at + count] - peak)
        weight_ref[:, at : at + count] = value
        mass = mass + value
    stats_ref[0:1, :] = peak
    stats_ref[1:2, :] = jnp.sum(mass, axis=0, keepdims=True)

    width = share_ref.shape[1]
    if width % 128 == 0:
        start = pl.multiple_of(lax.rem(lax.axis_index("dom") * width, fpix), width)
        share_ctf = ctf_ref[:, pl.ds(start, width)]
        share_ref[...] = share_ctf * share_ctf * inv_ref[:, pl.ds(start, width)]


def estep(images, refs, ctf, inv_noise, log_prior, shifts, rot_prior, groups, rpad, width):
    count, two_f = images.shape
    ngroup, fpix = ctf.shape
    nshift = shifts.shape[0]
    refs = jnp.swapaxes(refs, 0, 1)
    shifts = shifts.T
    return pl.pallas_call(
        estep_kernel,
        out_shape=(
            jax.ShapeDtypeStruct((rpad, nshift * count), F32),
            jax.ShapeDtypeStruct((nshift * count, two_f), BF16),
            jax.ShapeDtypeStruct((2, count), F32),
            jax.ShapeDtypeStruct((ngroup, count), F32),
            jax.ShapeDtypeStruct((ngroup, width), F32),
        ),
        in_specs=[HBM] * 8,
        out_specs=(VMEM,) * 5,
        scratch_shapes=[
            pltpu.VMEM(images.shape, images.dtype),
            pltpu.VMEM(refs.shape, refs.dtype),
            pltpu.VMEM(ctf.shape, F32),
            pltpu.VMEM(ctf.shape, F32),
            pltpu.VMEM(log_prior.shape, F32),
            pltpu.SMEM(shifts.shape, jnp.int32),
            pltpu.VMEM(rot_prior.shape, jnp.int32),
            pltpu.VMEM(groups.shape, jnp.int32),
            pltpu.VMEM((rpad, two_f), F32),
            pltpu.VMEM((rpad, two_f), BF16),
            pltpu.VMEM((count, fpix), F32),
            pltpu.VMEM((round_up(nshift, 8), fpix), F32),
            pltpu.VMEM((round_up(nshift, 8), fpix), F32),
            pltpu.SemaphoreType.DMA((8,)),
        ],
        compiler_params=PARAMS,
        name="estep",
    )(
        *(
            pltpu.with_memory_space_constraint(value, pltpu.HBM)
            for value in (images, refs, ctf, inv_noise, log_prior, shifts, rot_prior, groups)
        )
    )


def normaliser(stats_refs):
    parts = len(stats_refs)
    me = lax.axis_index("cls")
    stats = [ref[...] for ref in stats_refs]
    ordered = []
    for place in range(parts):
        value = stats[0]
        for ahead in range(1, parts):
            value = jnp.where(me ^ ahead == place, stats[ahead], value)
        ordered.append(value)
    peak = ordered[0][0:1]
    for value in ordered[1:]:
        peak = jnp.maximum(peak, value[0:1])
    total = jnp.zeros_like(peak)
    for value in ordered:
        total = total + value[1:2] * jnp.exp(value[0:1] - peak)
    loglik = peak + jnp.log(total)
    return loglik, jnp.exp(stats[0][0:1] - loglik)


def posterior(weight_ref, rows, scale, onehot_ref, post_ref):
    count = onehot_ref.shape[1]
    per_img = None
    for at in range(0, weight_ref.shape[1], count):
        post = (weight_ref[rows, at : at + count] * scale).astype(BF16)
        post_ref[rows, at : at + count] = post
        post = post.astype(F32)
        per_img = post if per_img is None else per_img + post
    three = jnp.concatenate([onehot_ref[...]] * 3, axis=1).astype(BF16)
    return lax.dot_general(
        three, thirds(per_img, 1), (((1,), (1,)), ((), ())), preferred_element_type=F32
    )


def class_sums(post_ref, copies_ref, rows, at, width):
    return jnp.dot(post_ref[rows, :], copies_ref[:, pl.ds(at, width)], preferred_element_type=F32)


LINE = 4
PAIR = 2
SLOW = 2_000_000_000
QUICK = 1000


def owner_column(place, mine, width):
    me = lax.axis_index("dom")
    z = me // PAIR
    y = me % PAIR
    low = z < 2
    stop = [
        jnp.where(low, 3, 0), jnp.where(low, 2, 1), jnp.where(low, 1 - z, 5 - z), z
    ][place]
    side = y if mine else 1 - y
    return pl.multiple_of((stop * PAIR + side) * width, width)


def put_mass(ref, mass):
    ngroup, hpad = mass.shape
    at = ref.shape[0] - ngroup
    ref[at:, 0:hpad] = mass
    ref[at:, hpad:] = jnp.zeros((ngroup, ref.shape[1] - hpad), F32)


def first_kernel(nstat, *refs):
    stats_refs = refs[:nstat]
    weight_ref, copies_ref, onehot_ref, post_ref, send_ref, scale_ref, loglik_ref = refs[nstat:]
    hpad = post_ref.shape[0]
    width = send_ref.shape[1]
    send = send_ref.shape[0] - onehot_ref.shape[0]
    rows = pl.ds(0, hpad)
    loglik, scale = normaliser(stats_refs)
    loglik_ref[...] = loglik.reshape(loglik.shape[1])
    scale_ref[...] = scale
    mass = posterior(weight_ref, rows, scale, onehot_ref, post_ref)
    sums = class_sums(post_ref, copies_ref, rows, owner_column(0, False, width), width)
    send_ref[0:send, :] = sums[0:send]
    put_mass(send_ref, mass)


def second_kernel(
    first_ref, scale_ref, weight_ref, copies_ref, onehot_ref, post_ref, send_ref, mass_ref
):
    hpad = post_ref.shape[0] // 2
    width = send_ref.shape[1]
    send = send_ref.shape[0] - onehot_ref.shape[0]
    rows = pl.ds(hpad, hpad)
    mass = posterior(weight_ref, rows, scale_ref[...], onehot_ref, post_ref)
    sums = class_sums(post_ref, copies_ref, rows, owner_column(0, False, width), width)
    send_ref[0:send, :] = sums[0:send]
    put_mass(send_ref, mass)
    put_mass(mass_ref, mass)
    post_ref[0:hpad, :] = first_ref[...]


def rest_kernel(post_ref, copies_ref, send_a_ref, mass_ref, *out_refs):
    hpad = post_ref.shape[0] // 2
    width = mass_ref.shape[1]
    chains = (out_refs[:6], out_refs[6:12])
    send = chains[0][1].shape[0]
    for place in (1, 0, 2, 3):
        for mine in (False, True):
            if place == 0 and not mine:
                continue
            at = owner_column(place, mine, width)

            @pl.when(at >= 0)
            def _(at=at, place=place, mine=mine):
                sums = class_sums(post_ref, copies_ref, pl.ds(0, 2 * hpad), at, width)
                for index, refs in enumerate(chains):
                    value = sums[index * hpad : index * hpad + send]
                    if place == 3 and not mine:
                        out_refs[12][index * send : (index + 1) * send, :] = value
                    else:
                        slot = (0, 1 + int(mine), 3 + int(mine), 5)[place]
                        refs[slot][0:send, :] = value

    chains[0][0][send:, :] = send_a_ref[send:, :]
    chains[1][0][send:, :] = mass_ref[...]


def last_kernel(chain, classes, rots, images, *refs):
    (keep_ref, pair_ref, own_ref, line_ref, cross_ref, share_ref), refs = refs[:6], refs[6:]
    before, refs = (refs[:2], refs[2:]) if chain else (None, refs)
    new_ref, frac_ref, ratio_ref = refs
    send, width = keep_ref.shape
    mine = rots // 2
    z = lax.axis_index("dom") // PAIR
    end = (z == 0) | (z == LINE - 1)
    mass = jnp.where(end, line_ref[send:, :], own_ref[send:, :])
    mass_high, mass_middle, mass_low = split(mass)
    high, middle, low = split(share_ref[...])
    den = lax.dot_general(
        jnp.concatenate([mass_high] * 3 + [mass_middle] * 2 + [mass_low], axis=0),
        jnp.concatenate([high, middle, low, high, middle, high], axis=0),
        (((0,), (0,)), ((), ())),
        preferred_element_type=F32,
    )
    num = keep_ref[...] + pair_ref[chain * send : (chain + 1) * send, :] + line_ref[0:send, :]
    num = num + jnp.where(end, 0.0, cross_ref[...])
    ratio_ref[0:send, :] = num / (den[0:send] + 1.0)
    ratio_ref[send:, :] = jnp.zeros((ratio_ref.shape[0] - send, width), F32)

    piece = 32
    per = 128 // piece
    kpad = round_up(classes, 8)
    lane = lax.broadcasted_iota(jnp.int32, (kpad, 128), 1)
    tiles = []
    values = [
        [ratio_ref[r * classes : r * classes + kpad, base : base + 128] for r in range(mine)]
        for base in range(0, width, 128)
    ]
    for chunk in range(0, width, piece):
        base = chunk // 128 * 128
        parts = []
        for r0 in range(0, mine, per):
            acc = jnp.zeros((kpad, 128), F32)
            for u in range(min(per, mine - r0)):
                turned = values[base // 128][r0 + u]
                turn = (u * piece - (chunk - base)) % 128
                if turn:
                    turned = pltpu.roll(turned, turn, 1)
                acc = jnp.where((lane >= u * piece) & (lane < (u + 1) * piece), turned, acc)
            parts.append(acc)
        tiles.append(jnp.concatenate(parts, axis=1))
    wide = piece * rots
    deep = tiles[0].shape[1]
    src = lax.broadcasted_iota(jnp.int32, (deep, wide), 0)
    dst = lax.broadcasted_iota(jnp.int32, (deep, wide), 1)
    src_r = src // piece
    perm = ((src - src_r * piece) * rots + src_r + chain * mine == dst) & (src_r < mine)
    moved = jnp.dot(
        thirds(jnp.concatenate(tiles, axis=0), 0), perm.astype(BF16), preferred_element_type=F32
    )
    count = len(tiles) * kpad
    moved = moved[0:count] + moved[count : 2 * count] + moved[2 * count :]
    for index in range(len(tiles)):
        columns = slice(index * wide, (index + 1) * wide)
        value = moved[index * kpad : index * kpad + classes, :]
        new_ref[:, columns] = value + before[0][:, columns] if before else value
    mrow = lax.broadcasted_iota(jnp.int32, (width, classes), 0)
    mcol = lax.broadcasted_iota(jnp.int32, (width, classes), 1)
    place = mrow.astype(F32)
    place = place - classes * jnp.floor((place + 0.5) * (1.0 / classes))
    member = ((place == mcol.astype(F32)) & (mrow < mine * classes)).astype(F32)
    share = jnp.dot(
        thirds(jnp.sum(mass, axis=0, keepdims=True), 0), member.astype(BF16),
        preferred_element_type=F32,
    )
    share = jnp.sum(share, axis=0, keepdims=True)
    if before:
        share = share + before[1][...]
        frac_ref[...] = (share / images).reshape(classes)
    else:
        frac_ref[...] = share


def line_path(stats, weight, copies, onehot, share, classes, rots, images):
    half = classes * rots // 2
    send = round_up(half, 8)
    ngroup, width = share.shape
    dom_n = lax.axis_size("dom")
    cls_n = lax.axis_size("cls")
    full = jax.ShapeDtypeStruct((send + ngroup, width), F32)
    body = jax.ShapeDtypeStruct((send, width), F32)
    mass_shape = jax.ShapeDtypeStruct((ngroup, width), F32)

    def first(*refs):
        first_kernel(len(stats), *refs)

    rpad, total = weight.shape
    count = onehot.shape[1]
    post_a, send_a, scale, loglik = pl.pallas_call(
        first,
        out_shape=(
            jax.ShapeDtypeStruct((rpad // 2, total), BF16),
            full,
            jax.ShapeDtypeStruct((1, count), F32),
            jax.ShapeDtypeStruct((count,), F32),
        ),
        in_specs=[VMEM] * (len(stats) + 3),
        out_specs=(VMEM,) * 4,
        compiler_params=PARAMS,
        name="first_sums",
    )(*stats, weight, copies, onehot)
    post, send_b, mass_b = pl.pallas_call(
        second_kernel,
        out_shape=(jax.ShapeDtypeStruct(weight.shape, BF16), full, mass_shape),
        in_specs=[VMEM] * 5,
        out_specs=(VMEM,) * 3,
        compiler_params=PARAMS,
        name="second_sums",
    )(post_a, scale, weight, copies, onehot)
    parts = pl.pallas_call(
        rest_kernel,
        out_shape=((full,) + (body,) * 5) * 2 + (jax.ShapeDtypeStruct((2 * send, width), F32),),
        in_specs=[VMEM] * 4,
        out_specs=(VMEM,) * 13,
        compiler_params=PARAMS,
        name="rest_sums",
    )(post, copies, send_a, mass_b)

    def along(pairs):
        return [(a * PAIR + y, b * PAIR + y) for a, b in pairs for y in range(PAIR)]

    across = [(d, d ^ 1) for d in range(dom_n)]
    outer = along([(0, 1), (1, 0), (2, 3), (3, 2)])
    facing = {0: 0, 1: 2, 2: 1, 3: 3}
    middle = [
        (
            (a * PAIR + y) * cls_n + c,
            (b * PAIR + y) * cls_n + (c if a != b else c ^ 1),
        )
        for a, b in facing.items()
        for y in range(PAIR)
        for c in range(cls_n)
    ]

    def swap(value):
        return lax.ppermute(value, "dom", across)

    def join(kernel, cost, out_shape, *values):
        return pl.pallas_call(
            kernel,
            out_shape=out_shape,
            in_specs=[VMEM] * len(values),
            out_specs=(VMEM,) * len(out_shape),
            compiler_params=PARAMS,
            cost_estimate=pl.CostEstimate(flops=cost, bytes_accessed=0, transcendentals=0),
            name="join",
        )(*values)

    def add2(left, right, out):
        out[...] = left[...] + right[...]

    def join1(keep1, pair1, sum0, got0, sum1, both0):
        sum1[...] = keep1[...] + pair1[...]
        both0[...] = sum0[...] + got0[...]

    def join2(keep2, pair2, sum1, got1, both0, got2, to_ends, to_middle):
        to_middle[...] = sum1[...] + got1[...]
        z = lax.axis_index("dom") // PAIR
        inner = (z != 0) & (z != LINE - 1)
        more = jnp.where(inner, got2[...], 0.0)
        to_ends[0:send, :] = keep2[...] + pair2[...] + more[0:send]
        to_ends[send:, :] = both0[send:, :] + more[send:]


    def reduce_chain(send0, keep0, send1, keep1, send2, keep2):
        pair0 = swap(send0)
        (sum0,) = join(add2, QUICK, (full,), keep0, pair0)
        send1, sum0 = lax.optimization_barrier((send1, sum0))
        pair1 = swap(send1)
        got0 = lax.ppermute(sum0, "dom", outer)
        sum1, both0 = join(join1, SLOW, (body, full), keep1, pair1, sum0, got0)
        send2, sum1, both0 = lax.optimization_barrier((send2, sum1, both0))
        pair2 = swap(send2)
        got1 = lax.ppermute(sum1, "dom", outer)
        got2 = lax.ppermute(both0, ("dom", "cls"), middle)
        to_ends, to_middle = join(
            join2, SLOW, (full, body), keep2, pair2, sum1, got1, both0, got2
        )
        line = lax.ppermute(to_ends, "dom", outer)
        cross = lax.ppermute(to_middle, ("dom", "cls"), middle)
        return pair2, to_ends, line, cross

    chain_a = reduce_chain(send_a, *parts[:5])
    chain_b = reduce_chain(send_b, *parts[6:11])
    send3, _ = lax.optimization_barrier((parts[12], chain_a[0]))
    pair3 = swap(send3)
    pieces_a = (parts[5], pair3) + chain_a[1:]
    pieces_b = (parts[11], pair3) + chain_b[1:]
    before = ()
    for chain, pieces in enumerate((pieces_a, pieces_b)):

        def last(*refs, chain=chain):
            last_kernel(chain, classes, rots, images, *refs)

        before = pl.pallas_call(
            last,
            out_shape=(
                jax.ShapeDtypeStruct((classes, width * rots), F32),
                jax.ShapeDtypeStruct((classes,) if chain else (1, classes), F32),
            ),
            in_specs=[VMEM] * (6 + len(before)),
            out_specs=(VMEM, VMEM),
            scratch_shapes=[pltpu.VMEM((send + 16, width), F32)],
            compiler_params=PARAMS,
            cost_estimate=pl.CostEstimate(flops=QUICK, bytes_accessed=0, transcendentals=0),
            name="last_ratio",
        )(*pieces, share, *before)
    return before[0], loglik, before[1]


def plain_path(stats, weight, copies, onehot, ctf, inv_noise, classes, rots, images):
    rpad = weight.shape[0]
    hpad = rpad // 2
    half = classes * rots // 2
    ngroup, fpix = ctf.shape
    two_f = 2 * fpix
    dom_n = lax.axis_size("dom")
    width = two_f // dom_n
    nstat = len(stats)

    def sums(*refs):
        weight_ref, copies_ref, onehot_ref, num_ref, mass_ref, loglik_ref, post_ref = refs[nstat:]
        loglik, scale = normaliser(refs[:nstat])
        loglik_ref[...] = loglik.reshape(loglik.shape[1])
        for index in range(2):
            rows = pl.ds(index * hpad, hpad)
            mass_ref[index] = posterior(weight_ref, rows, scale, onehot_ref, post_ref)
        for at in range(0, two_f, 256):
            num_ref[:, at : at + 256] = class_sums(
                post_ref, copies_ref, pl.ds(0, rpad), at, 256
            )

    num, mass, loglik = pl.pallas_call(
        sums,
        out_shape=(
            jax.ShapeDtypeStruct((rpad, two_f), F32),
            jax.ShapeDtypeStruct((2, ngroup, hpad), F32),
            jax.ShapeDtypeStruct(onehot.shape[1:], F32),
        ),
        in_specs=[VMEM] * (len(stats) + 3),
        out_specs=(VMEM,) * 3,
        scratch_shapes=[pltpu.VMEM(weight.shape, BF16)],
        compiler_params=PARAMS,
        name="all_sums",
    )(*stats, weight, copies, onehot)
    mass = jnp.concatenate([mass[0, :, :half], mass[1, :, :half]], axis=1)
    mass = lax.psum(mass, "dom")
    num = jnp.concatenate([num[:half], num[hpad : hpad + half]], axis=0)
    num = lax.psum_scatter(num, "dom", scatter_dimension=1, tiled=True)
    c2w = ctf * ctf * inv_noise
    c2w_two = jnp.concatenate([c2w, c2w], axis=1)
    c2w_part = lax.dynamic_slice_in_dim(c2w_two, lax.axis_index("dom") * width, width, 1)
    den = jnp.einsum("gn,gq->nq", mass, c2w_part, precision=HI)
    ratio = (num / (den + 1.0)).reshape(rots, classes, width)
    new_refs = ratio.transpose(1, 2, 0).reshape(classes, width * rots)
    frac = jnp.sum(mass.reshape(ngroup, rots, classes), axis=(0, 1)) / images
    return new_refs, loglik, frac


def local(images, refs, ctf, inv_noise, log_prior, shifts, rot_prior, groups):
    classes, rots, two_f = refs.shape
    half = classes * rots // 2
    hpad = round_up(half, 16)
    count = images.shape[0]
    ngroup = ctf.shape[0]
    dom_n = lax.axis_size("dom")
    cls_n = lax.axis_size("cls")
    width = two_f // dom_n
    weight, copies, stat, onehot, share = estep(
        images, refs, ctf, inv_noise, log_prior, shifts, rot_prior, groups, 2 * hpad, width
    )
    if cls_n & (cls_n - 1):
        raise ValueError("cls size")
    stats = [stat] + [
        lax.ppermute(stat, "cls", [(c, c ^ other) for c in range(cls_n)])
        for other in range(1, cls_n)
    ]
    fits = (
        dom_n == LINE * PAIR
        and cls_n % 2 == 0
        and width % 128 == 0
        and hpad <= width
        and ngroup % 8 == 0
    )
    images_n = count * dom_n
    if fits:
        return line_path(stats, weight, copies, onehot, share, classes, rots, images_n)
    return plain_path(stats, weight, copies, onehot, ctf, inv_noise, classes, rots, images_n)


def solution(mesh):
    return jax.shard_map(
        local,
        mesh=mesh,
        in_specs=(
            P("dom", None),
            P("cls", None, None),
            P(),
            P(),
            P("cls"),
            P(),
            P("dom"),
            P("dom"),
        ),
        out_specs=(P("cls", "dom"), P("dom"), P("cls")),
        check_vma=False,
    )
```
